32 devices in a mesh: expert: 16 (over z, x, core), tensor: 2 (over y).
Axes of the slice: x: 2, y: 2, z: 4, core: 2. Of those that a mesh axis runs over, the one named last changes fastest.
Arguments:
- tokens: bfloat16 [4096, 1024], P('expert'), may hold values from -6 to 6
- routes: int32 [4096, 2], P('expert'), may hold values from 0 to 15, all different within a row; in each aligned block of 256 rows (0 to 255, 256 to 511, ...) at most 64 rows name the same one
- mix_weights: float32 [4096, 2], P('expert'), may hold values from 0.2 to 1
- w_gate: bfloat16 [16, 1024, 2048], P('expert', None, 'tensor'), may hold values from -0.1875 to 0.1875
- w_up: bfloat16 [16, 1024, 2048], P('expert', None, 'tensor'), may hold values from -0.1875 to 0.1875
- w_down: bfloat16 [16, 2048, 1024], P('expert', 'tensor'), may hold values from -0.125 to 0.125
- cotangent: bfloat16 [4096, 1024], P('expert'), may hold values from -6 to 6
Outputs:
- result: bfloat16 [4096, 1024], P('expert')
- grad_tokens: bfloat16 [4096, 1024], P('expert')
- grad_gate: float32 [16, 1024, 2048], P('expert', None, 'tensor')
- grad_up: float32 [16, 1024, 2048], P('expert', None, 'tensor')
- grad_down: float32 [16, 2048, 1024], P('expert', 'tensor')
The draws below stay inside these ranges and needn't reach their ends.
Inputs may be any that keep to these rules, and one draw needn't show every extreme that they name: `routes`: each row names two different experts. Within each aligned block of 256 rows no expert is named by more than 64 rows, a bound that some block reaches.
All inputs are finite; a program needn't handle non-finite values.
Results may differ from the reference program's by a relative error of at most 0.015.
Values may be sent and summed in bfloat16 or wider, within the bound.
A program may use at most 128 MiB of HBM per device.

```python
import math
import jax
import jax.numpy as jnp
import numpy as np
from jax import lax

D = 1024
FF = 2048
TOK_DEV = 256
EXPERTS = 16
CAP = 64
TOKENS = 4096
N_EXPERT = 16
N_TENSOR = 2


def block_levels(key, dims, split, low, largest):
    def one(axis_at, blocks):
        draws = jax.random.uniform(jax.random.fold_in(jax.random.fold_in(key, 6), axis_at), (blocks,), jnp.float32, low / len(split), largest / len(split))
        return jnp.repeat(jnp.exp(draws), dims[axis_at] // blocks).reshape((-1,) + (1,) * (len(dims) - axis_at - 1))

    loudness = one(*split[0])
    for cut in split[1:]:
        loudness = loudness * one(*cut)
    return loudness


def routed_block(rng, own, number, rows, count, top, reach, slope):
    ranking = jax.random.permutation(rng, count)
    packed, ordinary = load_shares(count, rows * top, reach, slope, True), load_shares(count, rows * top, reach, slope, False)
    places = jnp.arange(count)

    def named(tallies, offset_by):
        used = int((tallies > 0).sum())
        fixed = max(1, used // 4)
        shifted = fixed + (places - fixed + offset_by * (used - fixed)) % max(1, count - fixed)
        return jnp.zeros((count,), jnp.int32).at[ranking[jnp.where(places < fixed, places, shifted)]].set(jnp.asarray(tallies, jnp.int32))

    tallies = jnp.where(number % 4 == 0, named(packed, number // 4), named(ordinary, number - number // 4 - 1))
    mixed = jax.random.permutation(jax.random.fold_in(own, 3), count)
    giver, taker = mixed[0:count // 2 * 2:2], mixed[1:count // 2 * 2:2]
    room = jnp.minimum(tallies[giver] - 1, reach - tallies[taker]) // 2
    room = jnp.where((giver == ranking[0]) | (taker == ranking[0]) | (tallies[taker] == 0), 0, jnp.maximum(room, 0))
    shifted = jax.random.randint(jax.random.fold_in(own, 4), (count // 2,), 0, 1 << 20) % (room + 1)
    tallies = tallies.at[giver].add(-shifted).at[taker].add(shifted)
    members = jnp.searchsorted(jnp.cumsum(tallies), jnp.arange(rows * top), side="right").astype(jnp.int32)
    listing = members.reshape(top, rows).T
    listing = listing[jax.random.permutation(jax.random.fold_in(own, 1), rows)]
    offset_by = jax.random.randint(jax.random.fold_in(own, 2), (rows, 1), 0, top)
    return jnp.take_along_axis(listing, (jnp.arange(top)[None, :] + offset_by) % top, axis=1)


def load_shares(count, total, bound, slope, full):
    weights = [(1 << 20) // math.isqrt(rank ** slope) + 1 for rank in range(1, count + 1)]
    largest = bound if full else min(bound, max(-(-total // count), total * weights[0] // sum(weights)))
    least = 1 if total - largest >= count - 1 else 0
    counts, rest = [largest] + [least] * (count - 1), total - largest - least * (count - 1)
    while rest > 0:
        movable = [i for i in range(1, count) if counts[i] < largest] or [i for i in range(1, count) if counts[i] < bound]
        pool, left = sum([weights[i] for i in movable]), rest
        for i in movable:
            extra = min(bound - counts[i], max(1, left * weights[i] // pool), rest)
            counts[i] = counts[i] + extra
            rest = rest - extra
    return np.array(counts)


def normal_values(rng, shape, width, most, split=(), kind=jnp.bfloat16):
    entries = jax.random.normal(rng, shape, jnp.float32) * width
    if len(split) > 0:
        entries = block_levels(rng, shape, split, -0.22, 0.18) * entries
    return jnp.clip(entries, min=-most, max=most).astype(kind)


def setup_inputs(seed: int = 0) -> dict:
    splits = jax.random.split(jax.random.key(seed), 8)
    tokens = normal_values(splits[0], (TOKENS, D), 1.0, 6.0, ((0, 16),))
    routes_keys = jax.random.split(jax.random.fold_in(splits[1], 1), TOKENS // TOK_DEV)
    routes_turns = jax.random.permutation(jax.random.fold_in(splits[1], 3), TOKENS // TOK_DEV)
    routes = jax.vmap(lambda own, number: routed_block(jax.random.fold_in(splits[1], 2), own, number, TOK_DEV, EXPERTS, 2, CAP, 2))(routes_keys, routes_turns).reshape((TOKENS, 2))
    mix_weights = jnp.clip(0.2 + 0.8 * jax.random.uniform(splits[2], (TOKENS, 2), jnp.float32) ** block_levels(splits[2], (TOKENS, 2), ((0, 16),), -0.2, 0.2), 0.2, 1.0)
    w_gate = normal_values(splits[3], (EXPERTS, D, FF), D ** -0.5, 0.1875, ((0, 16), (2, 2)))
    w_up = normal_values(splits[4], (EXPERTS, D, FF), D ** -0.5, 0.1875, ((0, 16), (2, 2)))
    w_down = normal_values(splits[5], (EXPERTS, FF, D), FF ** -0.5, 0.125, ((0, 16), (1, 2)))
    cotangent = normal_values(splits[6], (TOKENS, D), 1.0, 6.0, ((0, 16),))
    return {"tokens": tokens, "routes": routes, "mix_weights": mix_weights, "w_gate": w_gate, "w_up": w_up, "w_down": w_down, "cotangent": cotangent}


def expert_forward(received, gate_local, up_local, down_local):
    pre_gate = jnp.dot(received, gate_local, preferred_element_type=jnp.float32)
    pre_up = jnp.dot(received, up_local, preferred_element_type=jnp.float32)
    hidden = (jax.nn.silu(pre_gate) * pre_up).astype(jnp.bfloat16)
    partial_out = jnp.dot(hidden, down_local, preferred_element_type=jnp.float32)
    return pre_gate, pre_up, hidden, partial_out


def expert_backward(received, upstream, pre_gate, pre_up, hidden, gate_local, up_local, down_local):
    contract_last = (((1,), (1,)), ((), ()))
    contract_first = (((0,), (0,)), ((), ()))
    d_hidden = lax.dot_general(upstream, down_local, contract_last, preferred_element_type=jnp.float32)
    sigma = jax.nn.sigmoid(pre_gate)
    d_gate = (d_hidden * pre_up * sigma * (1.0 + pre_gate * (1.0 - sigma))).astype(jnp.bfloat16)
    d_up = (d_hidden * pre_gate * sigma).astype(jnp.bfloat16)
    grad_down = lax.dot_general(hidden, upstream, contract_first, preferred_element_type=jnp.float32)
    grad_gate = lax.dot_general(received, d_gate, contract_first, preferred_element_type=jnp.float32)
    grad_up = lax.dot_general(received, d_up, contract_first, preferred_element_type=jnp.float32)
    partial_in = lax.dot_general(d_gate, gate_local, contract_last, preferred_element_type=jnp.float32)
    partial_in = partial_in + lax.dot_general(d_up, up_local, contract_last, preferred_element_type=jnp.float32)
    return grad_gate, grad_up, grad_down, partial_in


def rounded(values):
    return lax.optimization_barrier(values.astype(jnp.bfloat16)).astype(jnp.float32)


def reference(tokens, routes, mix_weights, w_gate, w_up, w_down, cotangent):
    blocks = N_EXPERT
    group_width = FF // N_TENSOR
    route_blocks = routes.reshape(blocks, 2 * TOK_DEV)
    onehot = (route_blocks[:, :, None] == jnp.arange(EXPERTS, dtype=jnp.int32)[None, None, :]).astype(jnp.int32)
    slot_rank = jnp.sum((jnp.cumsum(onehot, axis=1) - 1) * onehot, axis=2)
    anchor = jnp.arange(blocks, dtype=jnp.int32)[:, None]
    slot_index = ((route_blocks * blocks + anchor) * CAP + slot_rank).reshape(-1).astype(jnp.int32)
    all_rows = EXPERTS * blocks * CAP
    doubled = jnp.repeat(tokens, 2, axis=0)
    x_buffer = jnp.zeros((all_rows, D), jnp.bfloat16).at[slot_index].set(doubled)
    x_buffer = x_buffer.reshape(EXPERTS, blocks * CAP, D)
    scaled = (mix_weights[:, :, None] * cotangent.astype(jnp.float32)[:, None, :]).astype(jnp.bfloat16)
    g_buffer = jnp.zeros((all_rows, D), jnp.bfloat16).at[slot_index].set(scaled.reshape(2 * TOKENS, D))
    g_buffer = g_buffer.reshape(EXPERTS, blocks * CAP, D)

    def per_expert(operands):
        received, upstream, gate_all, up_all, down_all = operands
        out_total = jnp.zeros((blocks * CAP, D), jnp.float32)
        in_total = jnp.zeros((blocks * CAP, D), jnp.float32)
        gate_parts, up_parts, down_parts = [], [], []
        for member in range(N_TENSOR):
            low = member * group_width
            gate_local = gate_all[:, low:low + group_width]
            up_local = up_all[:, low:low + group_width]
            down_local = down_all[low:low + group_width, :]
            pre_gate, pre_up, hidden, partial_out = expert_forward(received, gate_local, up_local, down_local)
            out_total = out_total + rounded(partial_out)
            grad_gate, grad_up, grad_down, partial_in = expert_backward(
                received, upstream, pre_gate, pre_up, hidden, gate_local, up_local, down_local)
            in_total = in_total + rounded(partial_in)
            gate_parts.append(grad_gate)
            up_parts.append(grad_up)
            down_parts.append(grad_down)
        return (out_total.astype(jnp.bfloat16), in_total.astype(jnp.bfloat16),
                jnp.concatenate(gate_parts, axis=1), jnp.concatenate(up_parts, axis=1),
                jnp.concatenate(down_parts, axis=0))

    out_buf, in_buf, grad_gate, grad_up, grad_down = lax.map(
        per_expert, (x_buffer, g_buffer, w_gate, w_up, w_down))
    out_flat = out_buf.reshape(all_rows, D)
    in_flat = in_buf.reshape(all_rows, D)
    picked = out_flat[slot_index].astype(jnp.float32).reshape(TOKENS, 2, D)
    result = jnp.sum(picked * mix_weights[:, :, None], axis=1).astype(jnp.bfloat16)
    picked_in = in_flat[slot_index].astype(jnp.float32).reshape(TOKENS, 2, D)
    ones_weights = jnp.ones_like(mix_weights)
    grad_tokens = jnp.sum(picked_in * ones_weights[:, :, None], axis=1).astype(jnp.bfloat16)
    return result, grad_tokens, grad_gate, grad_up, grad_down
```

```python
import functools

import jax
import jax.numpy as jnp
from jax import lax
from jax.experimental import pallas as pl
from jax.experimental.pallas import tpu as pltpu
from jax.sharding import PartitionSpec as P

MESH = pl.DeviceIdType.MESH
BF16 = jnp.bfloat16
F32 = jnp.float32
LAST = (((1,), (1,)), ((), ()))
FIRST = (((0,), (0,)), ((), ()))
GROUPS = 4
STEPS = range(GROUPS)


def dot(a, b):
    return jnp.dot(a, b, preferred_element_type=F32)


def dot_last(a, b):
    return lax.dot_general(a, b, LAST, preferred_element_type=F32)


def dot_first(a, b):
    return lax.dot_general(a, b, FIRST, preferred_element_type=F32)


def kernel(
    n_src, n_ten, cap,
    tok_ref, routes_ref, mix_ref, wg_hbm, wu_hbm, wd_hbm, cot_ref,
    res_ref, gtok_ref, gg_hbm, gu_hbm, gd_hbm,
    wg, wu, wd, pick, x_send, g_send, x_buf, g_buf, hidden, act_a, act_b, dg, du,
    part, part_in, arrived, arrived_in, ret, ret_in, back, back_in, halves, stage,
    w_sem, own_sem, x_ss, x_rs, g_ss, g_rs, xy_ss, xy_rs, gy_ss, gy_rs,
    p_ss, p_rs, q_ss, q_rs, o_ss, o_rs, i_ss, i_rs, f_ss, f_rs, st_sem,
):
    me = lax.axis_index("expert")
    ten = lax.axis_index("tensor")
    toks, width = tok_ref.shape
    part_w = width // n_ten
    ff = hidden.shape[1]
    tile = 256
    per = n_src // GROUPS
    grp = me // per
    mem = lax.rem(me, per)
    rows_g = per * cap
    partner = [grp, grp + 1 - 2 * lax.rem(grp, 2), lax.rem(grp + 2, 4), 3 - grp]

    def src_rows(s):
        return pl.ds(pl.multiple_of(s * cap, cap), cap)

    def grp_rows(j):
        return pl.ds(pl.multiple_of(partner[j] * rows_g, rows_g), rows_g)

    def members(j, body):
        def step(m, _):
            body(partner[j] * per + lax.rem(mem + m, per))
            return 0

        lax.fori_loop(1 if j == 0 else 0, per, step, 0)

    barrier = pltpu.get_barrier_semaphore()

    def greet(m, _):
        pl.semaphore_signal(
            barrier, inc=1, device_id=(lax.rem(me + m, n_src), ten), device_id_type=MESH
        )
        return 0

    lax.fori_loop(1, n_src, greet, 0)
    for o in range(1, n_ten):
        pl.semaphore_signal(
            barrier, inc=1, device_id=(me, lax.rem(ten + o, n_ten)), device_id_type=MESH
        )

    loads = [
        pltpu.make_async_copy(a, b, w_sem.at[i])
        for i, (a, b) in enumerate(((wg_hbm, wg), (wu_hbm, wu), (wd_hbm, wd)))
    ]
    for load in loads:
        load.start()

    lanes = lax.broadcasted_iota(jnp.int32, (toks, 128), 1)
    ones = [
        jnp.where(routes_ref[:, k:k + 1] == lanes, 1.0, 0.0).astype(F32) for k in range(2)
    ]
    before = jnp.where(
        lax.broadcasted_iota(jnp.int32, (toks, toks), 0)
        > lax.broadcasted_iota(jnp.int32, (toks, toks), 1), 1.0, 0.0
    ).astype(BF16)
    earlier = dot(before, (ones[0] + ones[1]).astype(BF16))
    places = lax.broadcasted_iota(jnp.int32, (toks, n_src * cap), 1)
    for k in range(2):
        rank = jnp.sum(ones[k] * earlier, axis=1, keepdims=True).astype(jnp.int32)
        place = routes_ref[:, k:k + 1] * cap + rank
        pick[k] = jnp.where(place == places, 1.0, 0.0).astype(BF16)

    my_cols = pl.ds(pl.multiple_of(ten * part_w, part_w), part_w)
    x_send[...] = dot_first(pick[0] + pick[1], tok_ref[:, my_cols]).astype(BF16)
    pl.semaphore_wait(barrier, n_src - 1 + n_ten - 1)

    def to_expert(buf_send, buf, ss, rs, e):
        return pltpu.make_async_remote_copy(
            src_ref=buf_send.at[src_rows(e)], dst_ref=buf.at[ten, src_rows(me)],
            send_sem=ss.at[e], recv_sem=rs.at[me], device_id=(e, ten), device_id_type=MESH,
        )

    def from_source(buf_send, buf, ss, rs, s):
        return pltpu.make_async_remote_copy(
            src_ref=buf_send.at[src_rows(s)], dst_ref=buf.at[ten, src_rows(s)],
            send_sem=ss.at[s], recv_sem=rs.at[s], device_id=(s, ten), device_id_type=MESH,
        )

    def send_all(buf_send, buf, ss, rs, i):
        own = pltpu.make_async_copy(
            buf_send.at[src_rows(me)], buf.at[ten, src_rows(me)], own_sem.at[i]
        )
        own.start()
        for j in (2, 3, 1, 0):
            members(j, lambda e: to_expert(buf_send, buf, ss, rs, e).start())
        return own

    own_x = send_all(x_send, x_buf, x_ss, x_rs, 0)
    cot = cot_ref[:, my_cols].astype(F32)
    scaled = [(mix_ref[:, k:k + 1] * cot).astype(BF16) for k in range(2)]
    g_send[...] = (dot_first(pick[0], scaled[0]) + dot_first(pick[1], scaled[1])).astype(BF16)
    own_g = send_all(g_send, g_buf, g_ss, g_rs, 1)

    def spread(buf, ss, rs, j, o):
        return pltpu.make_async_remote_copy(
            src_ref=buf.at[ten, grp_rows(j)], dst_ref=buf.at[ten, grp_rows(j)],
            send_sem=ss.at[o - 1, j], recv_sem=rs.at[o - 1, j],
            device_id=(me, lax.rem(ten + o, n_ten)), device_id_type=MESH,
        )

    def spread_in(buf, ss, rs, j, o):
        there = lax.rem(ten + n_ten - o, n_ten)
        return pltpu.make_async_remote_copy(
            src_ref=buf.at[ten, grp_rows(j)], dst_ref=buf.at[there, grp_rows(j)],
            send_sem=ss.at[o - 1, j], recv_sem=rs.at[o - 1, j],
            device_id=(me, there), device_id_type=MESH,
        )

    def exchange(buf, land, ss, rs, j, o):
        there = lax.rem(ten + o, n_ten)
        return pltpu.make_async_remote_copy(
            src_ref=buf.at[there, grp_rows(j)], dst_ref=land.at[o - 1, grp_rows(j)],
            send_sem=ss.at[o - 1, j], recv_sem=rs.at[o - 1, j],
            device_id=(me, there), device_id_type=MESH,
        )

    def to_source(buf, land, ss, rs, s):
        return pltpu.make_async_remote_copy(
            src_ref=buf.at[src_rows(s)], dst_ref=land.at[src_rows(me)],
            send_sem=ss.at[s], recv_sem=rs.at[me], device_id=(s, ten), device_id_type=MESH,
        )

    def from_expert(buf, land, ss, rs, e):
        return pltpu.make_async_remote_copy(
            src_ref=buf.at[src_rows(e)], dst_ref=land.at[src_rows(e)],
            send_sem=ss.at[e], recv_sem=rs.at[e], device_id=(e, ten), device_id_type=MESH,
        )

    def take(buf_send, buf, ss, rs, own, ys, yr, j):
        if j == 0:
            own.wait()
        members(j, lambda s: from_source(buf_send, buf, ss, rs, s).wait_recv())
        for o in range(1, n_ten):
            spread(buf, ys, yr, j, o).start()

    def joined(buf, ys, yr, j):
        for o in range(1, n_ten):
            spread_in(buf, ys, yr, j, o).wait_recv()

    def give(buf, land, ss, rs, j):
        for o in range(1, n_ten):
            exchange(buf, land, ss, rs, j, o).start()

    own_back = [None, None]

    def total_and_return(buf, land, ss, rs, out, final, oss, ors, j, i):
        for o in range(1, n_ten):
            exchange(buf, land, ss, rs, j, o).wait_recv()
        total = buf[ten, grp_rows(j), :].astype(F32)
        for o in range(1, n_ten):
            total = total + land[o - 1, grp_rows(j), :].astype(F32)
        out[grp_rows(j), :] = total.astype(BF16)
        if j == 0:
            own = pltpu.make_async_copy(
                out.at[src_rows(me)], final.at[src_rows(me)], own_sem.at[2 + i]
            )
            own.start()
            own_back[i] = own
        members(j, lambda s: to_source(out, final, oss, ors, s).start())

    def forward(j):
        rows = grp_rows(j)

        def step(n, _):
            cols = pl.ds(pl.multiple_of(n * tile, tile), tile)
            gate = jnp.zeros((rows_g, tile), F32)
            up = jnp.zeros((rows_g, tile), F32)
            for t in range(n_ten):
                deep = slice(t * part_w, (t + 1) * part_w)
                gate = gate + dot(x_buf[t, rows, :], wg[deep, cols])
                up = up + dot(x_buf[t, rows, :], wu[deep, cols])
            sigma = 1.0 / (1.0 + jnp.exp(-gate))
            silu = gate * sigma
            hidden[rows, cols] = (silu * up).astype(BF16)
            act_a[rows, cols] = up * sigma * (1.0 + gate * (1.0 - sigma))
            act_b[rows, cols] = silu
            return 0

        lax.fori_loop(0, ff // tile, step, 0)
        for t in range(n_ten):
            deep = slice(t * part_w, (t + 1) * part_w)
            part[t, rows, :] = dot(hidden[rows, :], wd[:, deep]).astype(BF16)

    def backward(j):
        rows = grp_rows(j)

        def step(n, _):
            cols = pl.ds(pl.multiple_of(n * tile, tile), tile)
            dh = jnp.zeros((rows_g, tile), F32)
            for t in range(n_ten):
                deep = slice(t * part_w, (t + 1) * part_w)
                dh = dh + dot_last(g_buf[t, rows, :], wd[cols, deep])
            dg[rows, cols] = (dh * act_a[rows, cols]).astype(BF16)
            du[rows, cols] = (dh * act_b[rows, cols]).astype(BF16)
            return 0

        lax.fori_loop(0, ff // tile, step, 0)
        for t in range(n_ten):
            deep = slice(t * part_w, (t + 1) * part_w)
            part_in[t, rows, :] = (
                dot_last(dg[rows, :], wg[deep, :]) + dot_last(du[rows, :], wu[deep, :])
            ).astype(BF16)

    out_args = (part, arrived, p_ss, p_rs, ret, back, o_ss, o_rs)
    in_args = (part_in, arrived_in, q_ss, q_rs, ret_in, back_in, i_ss, i_rs)

    for load in loads:
        load.wait()
    for j in range(GROUPS + 2):
        if j < GROUPS:
            take(x_send, x_buf, x_ss, x_rs, own_x, xy_ss, xy_rs, j)
        if j == GROUPS:
            take(g_send, g_buf, g_ss, g_rs, own_g, gy_ss, gy_rs, 0)
        if 1 <= j <= GROUPS:
            joined(x_buf, xy_ss, xy_rs, j - 1)
            forward(j - 1)
            give(part, arrived, p_ss, p_rs, j - 1)
        if j >= 2:
            total_and_return(*out_args, j - 2, 0)
    for j in range(1, GROUPS + 1):
        if j < GROUPS:
            take(g_send, g_buf, g_ss, g_rs, own_g, gy_ss, gy_rs, j)
        joined(g_buf, gy_ss, gy_rs, j - 1)
        backward(j - 1)
        give(part_in, arrived_in, q_ss, q_rs, j - 1)
        if j >= 2:
            total_and_return(*in_args, j - 2, 1)

    n_stage = ff // tile
    m_stage = width // tile

    def write(slot, dst):
        return pltpu.make_async_copy(stage.at[slot], dst, st_sem.at[slot])

    def grad_x(out_hbm, right, first):
        for m in range(m_stage):
            slot = m % 2
            t, low = (m * tile) // part_w, (m * tile) % part_w
            dst = out_hbm.at[pl.ds(m * tile, tile), :]
            if not (first and m < 2):
                pending[slot].wait()
            stage[slot, :, pl.ds(0, ff)] = dot_first(x_buf[t, :, low:low + tile], right[...])
            pending[slot] = pltpu.make_async_copy(
                stage.at[slot, :, pl.ds(0, ff)], dst, st_sem.at[slot]
            )
            pending[slot].start()

    pending = [None, None]

    def grad_hidden():
        for m in range(n_stage):
            slot = m % 2
            if pending[slot] is not None:
                pending[slot].wait()
            for t in range(n_ten):
                stage[slot, :, t * part_w:(t + 1) * part_w] = dot_first(
                    hidden[:, m * tile:(m + 1) * tile], g_buf[t]
                )
            pending[slot] = write(slot, gd_hbm.at[pl.ds(m * tile, tile), :])
            pending[slot].start()

    grad_hidden()
    total_and_return(*in_args, GROUPS - 1, 1)
    grad_x(gg_hbm, dg, False)
    grad_x(gu_hbm, du, False)

    def gathered(out, land, ss, rs, i, weights):
        sums = [jnp.zeros((toks, part_w), F32) for _ in range(2)]
        own_back[i].wait()
        for j in STEPS:
            members(j, lambda e: from_expert(out, land, ss, rs, e).wait_recv())
        for k in range(2):
            sums[k] = dot(pick[k], land[...])
            if weights is not None:
                sums[k] = weights[:, k:k + 1] * sums[k]
        halves[i, ten] = (sums[0] + sums[1]).astype(BF16)

    def share(i, o):
        return pltpu.make_async_remote_copy(
            src_ref=halves.at[i, ten], dst_ref=halves.at[i, ten],
            send_sem=f_ss.at[i, o - 1], recv_sem=f_rs.at[i, o - 1],
            device_id=(me, lax.rem(ten + o, n_ten)), device_id_type=MESH,
        )

    def share_in(i, o):
        there = lax.rem(ten + n_ten - o, n_ten)
        return pltpu.make_async_remote_copy(
            src_ref=halves.at[i, ten], dst_ref=halves.at[i, there],
            send_sem=f_ss.at[i, o - 1], recv_sem=f_rs.at[i, o - 1],
            device_id=(me, there), device_id_type=MESH,
        )

    gathered(ret, back, o_ss, o_rs, 0, mix_ref)
    for o in range(1, n_ten):
        share(0, o).start()
    gathered(ret_in, back_in, i_ss, i_rs, 1, None)
    for o in range(1, n_ten):
        share(1, o).start()
    for i, out in ((0, res_ref), (1, gtok_ref)):
        for o in range(1, n_ten):
            share_in(i, o).wait_recv()
        for t in range(n_ten):
            out[:, t * part_w:(t + 1) * part_w] = halves[i, t]

    for slot in range(2):
        pending[slot].wait()
    for j in STEPS:
        members(j, lambda e: to_expert(x_send, x_buf, x_ss, x_rs, e).wait_send())
        members(j, lambda e: to_expert(g_send, g_buf, g_ss, g_rs, e).wait_send())
        members(j, lambda s: to_source(ret, back, o_ss, o_rs, s).wait_send())
        members(j, lambda s: to_source(ret_in, back_in, i_ss, i_rs, s).wait_send())
        for o in range(1, n_ten):
            spread(x_buf, xy_ss, xy_rs, j, o).wait_send()
            spread(g_buf, gy_ss, gy_rs, j, o).wait_send()
            exchange(part, arrived, p_ss, p_rs, j, o).wait_send()
            exchange(part_in, arrived_in, q_ss, q_rs, j, o).wait_send()
    for i in range(2):
        for o in range(1, n_ten):
            share(i, o).wait_send()


def shards(tokens, routes, mix_weights, w_gate, w_up, w_down, cotangent):
    n_src = lax.axis_size("expert")
    n_ten = lax.axis_size("tensor")
    toks, width = tokens.shape
    ff = w_gate.shape[2]
    cap = 4 * toks // n_src
    rows = n_src * cap
    part_w = width // n_ten
    vmem = pl.BlockSpec(memory_space=pltpu.VMEM)
    hbm = pl.BlockSpec(memory_space=pl.ANY)
    dma = pltpu.SemaphoreType.DMA
    others = n_ten - 1
    scratch = [
        pltpu.VMEM((width, ff), BF16),
        pltpu.VMEM((width, ff), BF16),
        pltpu.VMEM((ff, width), BF16),
        pltpu.VMEM((2, toks, rows), BF16),
        pltpu.VMEM((rows, part_w), BF16),
        pltpu.VMEM((rows, part_w), BF16),
        pltpu.VMEM((n_ten, rows, part_w), BF16),
        pltpu.VMEM((n_ten, rows, part_w), BF16),
        pltpu.VMEM((rows, ff), BF16),
        pltpu.VMEM((rows, ff), F32),
        pltpu.VMEM((rows, ff), F32),
        pltpu.VMEM((rows, ff), BF16),
        pltpu.VMEM((rows, ff), BF16),
        pltpu.VMEM((n_ten, rows, part_w), BF16),
        pltpu.VMEM((n_ten, rows, part_w), BF16),
        pltpu.VMEM((others, rows, part_w), BF16),
        pltpu.VMEM((others, rows, part_w), BF16),
        pltpu.VMEM((rows, part_w), BF16),
        pltpu.VMEM((rows, part_w), BF16),
        pltpu.VMEM((rows, part_w), BF16),
        pltpu.VMEM((rows, part_w), BF16),
        pltpu.VMEM((2, n_ten, toks, part_w), BF16),
        pltpu.VMEM((2, 256, width), F32),
        dma((3,)),
        dma((4,)),
        dma((n_src,)), dma((n_src,)), dma((n_src,)), dma((n_src,)),
        dma((others, GROUPS)), dma((others, GROUPS)), dma((others, GROUPS)), dma((others, GROUPS)),
        dma((others, GROUPS)), dma((others, GROUPS)), dma((others, GROUPS)), dma((others, GROUPS)),
        dma((n_src,)), dma((n_src,)), dma((n_src,)), dma((n_src,)),
        dma((2, others)), dma((2, others)),
        dma((2,)),
    ]
    result, grad_tokens, gg, gu, gd = pl.pallas_call(
        functools.partial(kernel, n_src, n_ten, cap),
        out_shape=(
            jax.ShapeDtypeStruct((toks, width), BF16),
            jax.ShapeDtypeStruct((toks, width), BF16),
            jax.ShapeDtypeStruct((width, ff), F32),
            jax.ShapeDtypeStruct((width, ff), F32),
            jax.ShapeDtypeStruct((ff, width), F32),
        ),
        in_specs=[vmem, vmem, vmem, hbm, hbm, hbm, vmem],
        out_specs=(vmem, vmem, hbm, hbm, hbm),
        scratch_shapes=scratch,
        compiler_params=pltpu.CompilerParams(
            collective_id=0, has_side_effects=True, vmem_limit_bytes=56 * 2**20
        ),
        cost_estimate=pl.CostEstimate(
            flops=18 * rows * width * ff, bytes_accessed=20 * width * ff,
            transcendentals=rows * ff,
        ),
    )(tokens, routes, mix_weights, w_gate[0], w_up[0], w_down[0], cotangent)
    return result, grad_tokens, gg[None], gu[None], gd[None]


def solution(mesh):
    in_specs = (
        P("expert", None),
        P("expert", None),
        P("expert", None),
        P("expert", None, "tensor"),
        P("expert", None, "tensor"),
        P("expert", "tensor", None),
        P("expert", None),
    )
    out_specs = (
        P("expert", None),
        P("expert", None),
        P("expert", None, "tensor"),
        P("expert", None, "tensor"),
        P("expert", "tensor", None),
    )
    return jax.shard_map(shards, mesh=mesh, in_specs=in_specs, out_specs=out_specs, check_vma=False)
```

```python
import functools

import jax
import jax.numpy as jnp
from jax import lax
from jax.experimental import pallas as pl
from jax.experimental.pallas import tpu as pltpu
from jax.sharding import PartitionSpec as P

MESH = pl.DeviceIdType.MESH
BF16 = jnp.bfloat16
F32 = jnp.float32
LAST = (((1,), (1,)), ((), ()))
FIRST = (((0,), (0,)), ((), ()))
GROUPS = 4
NEAR = 2
STEPS = range(GROUPS)


def dot(a, b):
    return jnp.dot(a, b, preferred_element_type=F32)


def dot_last(a, b):
    return lax.dot_general(a, b, LAST, preferred_element_type=F32)


def dot_first(a, b):
    return lax.dot_general(a, b, FIRST, preferred_element_type=F32)


def kernel(
    n_src, n_ten, cap,
    tok_hbm, routes_ref, mix_ref, wg_hbm, wu_hbm, wd_hbm, cot_hbm,
    res_ref, gtok_ref, gg_hbm, gu_hbm, gd_hbm,
    tok_ref, cot_ref, wg, wu, wd, pick, x_send, g_send, x_buf, g_buf, hidden, act_a, act_b, dg, du,
    part, part_in, arrived, arrived_in, ret, ret_in, back, back_in, near, near_in, halves, stage,
    w_sem, own_sem, x_ss, x_rs, g_ss, g_rs, xy_ss, xy_rs, gy_ss, gy_rs,
    p_ss, p_rs, q_ss, q_rs, o_ss, o_rs, i_ss, i_rs, f_ss, f_rs, c_ss, c_rs, st_sem,
):
    me = lax.axis_index("expert")
    ten = lax.axis_index("tensor")
    toks, width = tok_ref.shape
    part_w = width // n_ten
    ff = hidden.shape[1]
    tile = 256
    per = n_src // GROUPS
    grp = me // per
    mem = lax.rem(me, per)
    rows_g = per * cap
    partner = [grp, grp + 1 - 2 * lax.rem(grp, 2), lax.rem(grp + 2, 4), 3 - grp]

    def src_rows(s):
        return pl.ds(pl.multiple_of(s * cap, cap), cap)

    def grp_rows(j):
        return pl.ds(pl.multiple_of(partner[j] * rows_g, rows_g), rows_g)

    def members(j, body):
        def step(m, _):
            body(partner[j] * per + lax.rem(mem + m, per))
            return 0

        lax.fori_loop(1 if j == 0 else 0, per, step, 0)

    barrier = pltpu.get_barrier_semaphore()

    def greet(m, _):
        pl.semaphore_signal(
            barrier, inc=1, device_id=(lax.rem(me + m, n_src), ten), device_id_type=MESH
        )
        return 0

    lax.fori_loop(1, n_src, greet, 0)
    for o in range(1, n_ten):
        pl.semaphore_signal(
            barrier, inc=1, device_id=(me, lax.rem(ten + o, n_ten)), device_id_type=MESH
        )

    loads = [
        pltpu.make_async_copy(a, b, w_sem.at[i])
        for i, (a, b) in enumerate((
            (tok_hbm, tok_ref), (cot_hbm, cot_ref), (wg_hbm, wg), (wu_hbm, wu), (wd_hbm, wd)
        ))
    ]
    for load in loads:
        load.start()

    experts = lax.broadcasted_iota(jnp.int32, (128, toks), 0)
    ones = [
        jnp.where(routes_ref[k:k + 1, :] == experts, 1.0, 0.0).astype(F32) for k in range(2)
    ]
    down = lax.broadcasted_iota(jnp.int32, (toks, toks), 0)
    across = lax.broadcasted_iota(jnp.int32, (toks, toks), 1)
    before = jnp.where(down < across, 1.0, 0.0).astype(BF16)
    earlier = dot((ones[0] + ones[1]).astype(BF16), before)
    places = lax.broadcasted_iota(jnp.int32, (n_src * cap, toks), 0)
    place = [
        routes_ref[k:k + 1, :] * cap
        + jnp.sum(ones[k] * earlier, axis=0, keepdims=True).astype(jnp.int32)
        for k in range(2)
    ]
    held = [place[k] == places for k in range(2)]
    spots = (jnp.where(held[0], 1.0, 0.0) + jnp.where(held[1], 1.0, 0.0)).astype(BF16)

    def columns(t):
        return slice(t * part_w, (t + 1) * part_w)

    loads[0].wait()
    for t in range(n_ten):
        x_send[t] = dot(spots, tok_ref[:, columns(t)]).astype(BF16)
    pl.semaphore_wait(barrier, n_src - 1 + n_ten - 1)

    def halves_of(j):
        return slice(None) if j < NEAR else ten

    def to_expert(buf_send, buf, ss, rs, j, e):
        return pltpu.make_async_remote_copy(
            src_ref=buf_send.at[halves_of(j), src_rows(e)],
            dst_ref=buf.at[halves_of(j), src_rows(me)],
            send_sem=ss.at[e], recv_sem=rs.at[me], device_id=(e, ten), device_id_type=MESH,
        )

    def from_source(buf_send, buf, ss, rs, j, s):
        return pltpu.make_async_remote_copy(
            src_ref=buf_send.at[halves_of(j), src_rows(s)],
            dst_ref=buf.at[halves_of(j), src_rows(s)],
            send_sem=ss.at[s], recv_sem=rs.at[s], device_id=(s, ten), device_id_type=MESH,
        )

    def send_all(buf_send, buf, ss, rs, i):
        own = pltpu.make_async_copy(
            buf_send.at[:, src_rows(me)], buf.at[:, src_rows(me)], own_sem.at[i]
        )
        own.start()

        def to(j, m):
            e = partner[j] * per + lax.rem(mem + m, per)
            to_expert(buf_send, buf, ss, rs, j, e).start()

        def step(m, _):
            for j in (2, 0, 3, 1):
                to(j, m)
            return 0

        for j in (2, 3, 1):
            to(j, 0)
        lax.fori_loop(1, per, step, 0)
        return own

    own_x = send_all(x_send, x_buf, x_ss, x_rs, 0)
    weight = jnp.sum(
        jnp.where(held[0], mix_ref[0:1, :], 0.0) + jnp.where(held[1], mix_ref[1:2, :], 0.0),
        axis=1, keepdims=True,
    )
    loads[1].wait()
    for t in range(n_ten):
        g_send[t] = (weight * dot(spots, cot_ref[:, columns(t)])).astype(BF16)
    own_g = send_all(g_send, g_buf, g_ss, g_rs, 1)

    def upright(row):
        return jnp.sum(jnp.where(down == across, row, 0.0), axis=1, keepdims=True)

    lanes = lax.broadcasted_iota(jnp.int32, (toks, n_src * cap), 1)
    for k in range(2):
        column = upright(place[k].astype(F32)).astype(jnp.int32)
        pick[k] = jnp.where(column == lanes, 1.0, 0.0).astype(BF16)
    mix = [upright(mix_ref[k:k + 1, :]) for k in range(2)]

    def spread(buf, ss, rs, j, o):
        return pltpu.make_async_remote_copy(
            src_ref=buf.at[ten, grp_rows(j)], dst_ref=buf.at[ten, grp_rows(j)],
            send_sem=ss.at[o - 1, j], recv_sem=rs.at[o - 1, j],
            device_id=(me, lax.rem(ten + o, n_ten)), device_id_type=MESH,
        )

    def spread_in(buf, ss, rs, j, o):
        there = lax.rem(ten + n_ten - o, n_ten)
        return pltpu.make_async_remote_copy(
            src_ref=buf.at[ten, grp_rows(j)], dst_ref=buf.at[there, grp_rows(j)],
            send_sem=ss.at[o - 1, j], recv_sem=rs.at[o - 1, j],
            device_id=(me, there), device_id_type=MESH,
        )

    def exchange(buf, land, ss, rs, j, o):
        there = lax.rem(ten + o, n_ten)
        return pltpu.make_async_remote_copy(
            src_ref=buf.at[there, grp_rows(j)], dst_ref=land.at[o - 1, grp_rows(j)],
            send_sem=ss.at[o - 1, j], recv_sem=rs.at[o - 1, j],
            device_id=(me, there), device_id_type=MESH,
        )

    def to_source(buf, out, land, ss, rs, j, s):
        src = buf.at[:, src_rows(s)] if j < NEAR else out.at[src_rows(s)]
        return pltpu.make_async_remote_copy(
            src_ref=src, dst_ref=land.at[halves_of(j), src_rows(me)],
            send_sem=ss.at[s], recv_sem=rs.at[me], device_id=(s, ten), device_id_type=MESH,
        )

    def from_expert(buf, out, land, ss, rs, j, e):
        src = buf.at[:, src_rows(e)] if j < NEAR else out.at[src_rows(e)]
        return pltpu.make_async_remote_copy(
            src_ref=src, dst_ref=land.at[halves_of(j), src_rows(e)],
            send_sem=ss.at[e], recv_sem=rs.at[e], device_id=(e, ten), device_id_type=MESH,
        )

    def take(buf_send, buf, ss, rs, own, ys, yr, j):
        if j == 0:
            own.wait()
        members(j, lambda s: from_source(buf_send, buf, ss, rs, j, s).wait_recv())
        if j >= NEAR:
            for o in range(1, n_ten):
                spread(buf, ys, yr, j, o).start()

    def joined(buf, ys, yr, j):
        if j >= NEAR:
            for o in range(1, n_ten):
                spread_in(buf, ys, yr, j, o).wait_recv()

    own_back = [None, None]

    def give(buf, land, ss, rs, out, final, oss, ors, j, i):
        if j >= NEAR:
            for o in range(1, n_ten):
                exchange(buf, land, ss, rs, j, o).start()
            return
        if j == 0:
            own_back[i] = pltpu.make_async_copy(
                buf.at[:, src_rows(me)], final.at[:, src_rows(me)], own_sem.at[2 + i]
            )
            own_back[i].start()
        members(j, lambda s: to_source(buf, out, final, oss, ors, j, s).start())

    def total_and_return(buf, land, ss, rs, out, final, oss, ors, j):
        for o in range(1, n_ten):
            exchange(buf, land, ss, rs, j, o).wait_recv()
        total = buf[ten, grp_rows(j), :].astype(F32)
        for o in range(1, n_ten):
            total = total + land[o - 1, grp_rows(j), :].astype(F32)
        out[grp_rows(j), :] = total.astype(BF16)
        members(j, lambda s: to_source(buf, out, final, oss, ors, j, s).start())

    def forward(j):
        rows = grp_rows(j)

        def step(n, _):
            cols = pl.ds(pl.multiple_of(n * tile, tile), tile)
            gate = jnp.zeros((rows_g, tile), F32)
            up = jnp.zeros((rows_g, tile), F32)
            for t in range(n_ten):
                deep = slice(t * part_w, (t + 1) * part_w)
                gate = gate + dot(x_buf[t, rows, :], wg[deep, cols])
                up = up + dot(x_buf[t, rows, :], wu[deep, cols])
            sigma = 1.0 / (1.0 + jnp.exp(-gate))
            silu = gate * sigma
            hidden[rows, cols] = (silu * up).astype(BF16)
            act_a[rows, cols] = up * sigma * (1.0 + gate * (1.0 - sigma))
            act_b[rows, cols] = silu
            return 0

        lax.fori_loop(0, ff // tile, step, 0)
        for t in range(n_ten):
            deep = slice(t * part_w, (t + 1) * part_w)
            part[t, rows, :] = dot(hidden[rows, :], wd[:, deep]).astype(BF16)

    def backward(j):
        rows = grp_rows(j)

        def step(n, _):
            cols = pl.ds(pl.multiple_of(n * tile, tile), tile)
            dh = jnp.zeros((rows_g, tile), F32)
            for t in range(n_ten):
                deep = slice(t * part_w, (t + 1) * part_w)
                dh = dh + dot_last(g_buf[t, rows, :], wd[cols, deep])
            dg[rows, cols] = (dh * act_a[rows, cols]).astype(BF16)
            du[rows, cols] = (dh * act_b[rows, cols]).astype(BF16)
            return 0

        lax.fori_loop(0, ff // tile, step, 0)
        for t in range(n_ten):
            deep = slice(t * part_w, (t + 1) * part_w)
            part_in[t, rows, :] = (
                dot_last(dg[rows, :], wg[deep, :]) + dot_last(du[rows, :], wu[deep, :])
            ).astype(BF16)

    out_args = (part, arrived, p_ss, p_rs, ret, back, o_ss, o_rs)
    in_args = (part_in, arrived_in, q_ss, q_rs, ret_in, back_in, i_ss, i_rs)

    for load in loads[2:]:
        load.wait()
    for j in STEPS:
        take(x_send, x_buf, x_ss, x_rs, own_x, xy_ss, xy_rs, j)
        if j >= 1:
            joined(x_buf, xy_ss, xy_rs, j - 1)
            forward(j - 1)
            give(*out_args, j - 1, 0)
    joined(x_buf, xy_ss, xy_rs, 3)
    forward(3)
    give(*out_args, 3, 0)
    total_and_return(*out_args, 2)
    take(g_send, g_buf, g_ss, g_rs, own_g, gy_ss, gy_rs, 0)
    take(g_send, g_buf, g_ss, g_rs, own_g, gy_ss, gy_rs, 1)
    backward(0)
    give(*in_args, 0, 1)
    total_and_return(*out_args, 3)
    take(g_send, g_buf, g_ss, g_rs, own_g, gy_ss, gy_rs, 2)
    backward(1)
    give(*in_args, 1, 1)
    take(g_send, g_buf, g_ss, g_rs, own_g, gy_ss, gy_rs, 3)
    for j in (2, 3):
        joined(g_buf, gy_ss, gy_rs, j)
        backward(j)
        give(*in_args, j, 1)
    total_and_return(*in_args, 2)

    n_stage = ff // tile
    m_stage = width // tile

    def write(slot, dst):
        return pltpu.make_async_copy(stage.at[slot], dst, st_sem.at[slot])

    def grad_x(out_hbm, right, first):
        for m in range(m_stage):
            slot = m % 2
            t, low = (m * tile) // part_w, (m * tile) % part_w
            dst = out_hbm.at[pl.ds(m * tile, tile), :]
            if not (first and m < 2):
                pending[slot].wait()
            stage[slot, :, pl.ds(0, ff)] = dot_first(
                x_buf[t, :, low:low + tile], right[...]
            ).astype(BF16)
            pending[slot] = pltpu.make_async_copy(
                stage.at[slot, :, pl.ds(0, ff)], dst, st_sem.at[slot]
            )
            pending[slot].start()

    pending = [None, None]

    def grad_hidden():
        for m in range(n_stage):
            slot = m % 2
            if pending[slot] is not None:
                pending[slot].wait()
            for t in range(n_ten):
                stage[slot, :, t * part_w:(t + 1) * part_w] = dot_first(
                    hidden[:, m * tile:(m + 1) * tile], g_buf[t]
                ).astype(BF16)
            pending[slot] = write(slot, gd_hbm.at[pl.ds(m * tile, tile), :])
            pending[slot].start()

    def picked(land, weights, j, t):
        rows = grp_rows(j)
        terms = [dot(pick[k, :, rows], land[t, rows, :]) for k in range(2)]
        if weights is not None:
            terms = [weights[k] * terms[k] for k in range(2)]
        return terms[0] + terms[1]

    def swap(i, o):
        there = lax.rem(ten + o, n_ten)
        return pltpu.make_async_remote_copy(
            src_ref=near.at[i, there], dst_ref=near_in.at[i, o - 1],
            send_sem=c_ss.at[i, o - 1], recv_sem=c_rs.at[i, o - 1],
            device_id=(me, there), device_id_type=MESH,
        )

    def gather_near(args, i, weights):
        buf, land, _, _, out, final, oss, ors = args
        own_back[i].wait()
        for j in range(NEAR):
            members(j, lambda e: from_expert(buf, out, final, oss, ors, j, e).wait_recv())
        for t in range(n_ten):
            total = picked(final, weights, 0, t)
            for j in range(1, NEAR):
                total = total + picked(final, weights, j, t)
            near[i, t] = total.astype(BF16)
        for o in range(1, n_ten):
            swap(i, o).start()

    def gather_far(args, i, weights):
        buf, land, _, _, out, final, oss, ors = args
        for o in range(1, n_ten):
            swap(i, o).wait_recv()
        total = near[i, ten].astype(F32)
        for o in range(1, n_ten):
            total = total + near_in[i, o - 1].astype(F32)
        for j in range(NEAR, GROUPS):
            members(j, lambda e: from_expert(buf, out, final, oss, ors, j, e).wait_recv())
            total = total + picked(final, weights, j, ten)
        halves[i, ten] = total.astype(BF16)
        for o in range(1, n_ten):
            share(i, o).start()

    def share(i, o):
        return pltpu.make_async_remote_copy(
            src_ref=halves.at[i, ten], dst_ref=halves.at[i, ten],
            send_sem=f_ss.at[i, o - 1], recv_sem=f_rs.at[i, o - 1],
            device_id=(me, lax.rem(ten + o, n_ten)), device_id_type=MESH,
        )

    def share_in(i, o):
        there = lax.rem(ten + n_ten - o, n_ten)
        return pltpu.make_async_remote_copy(
            src_ref=halves.at[i, ten], dst_ref=halves.at[i, there],
            send_sem=f_ss.at[i, o - 1], recv_sem=f_rs.at[i, o - 1],
            device_id=(me, there), device_id_type=MESH,
        )

    grad_hidden()
    total_and_return(*in_args, 3)
    gather_near(out_args, 0, mix)
    grad_x(gg_hbm, dg, False)
    gather_near(in_args, 1, None)
    gather_far(out_args, 0, mix)
    grad_x(gu_hbm, du, False)
    gather_far(in_args, 1, None)
    for i, out in ((0, res_ref), (1, gtok_ref)):
        for o in range(1, n_ten):
            share_in(i, o).wait_recv()
        for t in range(n_ten):
            out[:, t * part_w:(t + 1) * part_w] = halves[i, t]

    for slot in range(2):
        pending[slot].wait()
    for j in STEPS:
        members(j, lambda e: to_expert(x_send, x_buf, x_ss, x_rs, j, e).wait_send())
        members(j, lambda e: to_expert(g_send, g_buf, g_ss, g_rs, j, e).wait_send())
        for buf, _, _, _, out, final, oss, ors in (out_args, in_args):
            members(j, lambda s: to_source(buf, out, final, oss, ors, j, s).wait_send())
        if j >= NEAR:
            for o in range(1, n_ten):
                spread(x_buf, xy_ss, xy_rs, j, o).wait_send()
                spread(g_buf, gy_ss, gy_rs, j, o).wait_send()
                exchange(part, arrived, p_ss, p_rs, j, o).wait_send()
                exchange(part_in, arrived_in, q_ss, q_rs, j, o).wait_send()
    for i in range(2):
        for o in range(1, n_ten):
            share(i, o).wait_send()
            swap(i, o).wait_send()


def shards(tokens, routes, mix_weights, w_gate, w_up, w_down, cotangent):
    n_src = lax.axis_size("expert")
    n_ten = lax.axis_size("tensor")
    toks, width = tokens.shape
    ff = w_gate.shape[2]
    cap = 4 * toks // n_src
    rows = n_src * cap
    part_w = width // n_ten
    vmem = pl.BlockSpec(memory_space=pltpu.VMEM)
    hbm = pl.BlockSpec(memory_space=pl.ANY)
    dma = pltpu.SemaphoreType.DMA
    others = n_ten - 1
    scratch = [
        pltpu.VMEM((toks, width), BF16),
        pltpu.VMEM((toks, width), BF16),
        pltpu.VMEM((width, ff), BF16),
        pltpu.VMEM((width, ff), BF16),
        pltpu.VMEM((ff, width), BF16),
        pltpu.VMEM((2, toks, rows), BF16),
        pltpu.VMEM((n_ten, rows, part_w), BF16),
        pltpu.VMEM((n_ten, rows, part_w), BF16),
        pltpu.VMEM((n_ten, rows, part_w), BF16),
        pltpu.VMEM((n_ten, rows, part_w), BF16),
        pltpu.VMEM((rows, ff), BF16),
        pltpu.VMEM((rows, ff), F32),
        pltpu.VMEM((rows, ff), F32),
        pltpu.VMEM((rows, ff), BF16),
        pltpu.VMEM((rows, ff), BF16),
        pltpu.VMEM((n_ten, rows, part_w), BF16),
        pltpu.VMEM((n_ten, rows, part_w), BF16),
        pltpu.VMEM((others, rows, part_w), BF16),
        pltpu.VMEM((others, rows, part_w), BF16),
        pltpu.VMEM((rows, part_w), BF16),
        pltpu.VMEM((rows, part_w), BF16),
        pltpu.VMEM((n_ten, rows, part_w), BF16),
        pltpu.VMEM((n_ten, rows, part_w), BF16),
        pltpu.VMEM((2, n_ten, toks, part_w), BF16),
        pltpu.VMEM((2, others, toks, part_w), BF16),
        pltpu.VMEM((2, n_ten, toks, part_w), BF16),
        pltpu.VMEM((2, 256, width), BF16),
        dma((5,)),
        dma((4,)),
        dma((n_src,)), dma((n_src,)), dma((n_src,)), dma((n_src,)),
        dma((others, GROUPS)), dma((others, GROUPS)), dma((others, GROUPS)), dma((others, GROUPS)),
        dma((others, GROUPS)), dma((others, GROUPS)), dma((others, GROUPS)), dma((others, GROUPS)),
        dma((n_src,)), dma((n_src,)), dma((n_src,)), dma((n_src,)),
        dma((2, others)), dma((2, others)), dma((2, others)), dma((2, others)),
        dma((2,)),
    ]
    result, grad_tokens, gg, gu, gd = pl.pallas_call(
        functools.partial(kernel, n_src, n_ten, cap),
        out_shape=(
            jax.ShapeDtypeStruct((toks, width), BF16),
            jax.ShapeDtypeStruct((toks, width), BF16),
            jax.ShapeDtypeStruct((width, ff), BF16),
            jax.ShapeDtypeStruct((width, ff), BF16),
            jax.ShapeDtypeStruct((ff, width), BF16),
        ),
        in_specs=[hbm, vmem, vmem, hbm, hbm, hbm, hbm],
        out_specs=(vmem, vmem, hbm, hbm, hbm),
        scratch_shapes=scratch,
        compiler_params=pltpu.CompilerParams(
            collective_id=0, has_side_effects=True, vmem_limit_bytes=60 * 2**20
        ),
        cost_estimate=pl.CostEstimate(
            flops=18 * rows * width * ff, bytes_accessed=20 * width * ff,
            transcendentals=rows * ff,
        ),
    )(tokens, routes.T, mix_weights.T, w_gate[0], w_up[0], w_down[0], cotangent)
    return result, grad_tokens, gg[None].astype(F32), gu[None].astype(F32), gd[None].astype(F32)


def solution(mesh):
    in_specs = (
        P("expert", None),
        P("expert", None),
        P("expert", None),
        P("expert", None, "tensor"),
        P("expert", None, "tensor"),
        P("expert", "tensor", None),
        P("expert", None),
    )
    out_specs = (
        P("expert", None),
        P("expert", None),
        P("expert", None, "tensor"),
        P("expert", None, "tensor"),
        P("expert", "tensor", None),
    )
    return jax.shard_map(shards, mesh=mesh, in_specs=in_specs, out_specs=out_specs, check_vma=False)
```

```python
import functools

import jax
import jax.numpy as jnp
from jax import lax
from jax.experimental import pallas as pl
from jax.experimental.pallas import tpu as pltpu
from jax.sharding import PartitionSpec as P

MESH = pl.DeviceIdType.MESH
BF16 = jnp.bfloat16
F32 = jnp.float32
LAST = (((1,), (1,)), ((), ()))
FIRST = (((0,), (0,)), ((), ()))
GROUPS = 4
NEAR = 2
STEPS = range(GROUPS)


def dot(a, b):
    return jnp.dot(a, b, preferred_element_type=F32)


def dot_last(a, b):
    return lax.dot_general(a, b, LAST, preferred_element_type=F32)


def dot_first(a, b):
    return lax.dot_general(a, b, FIRST, preferred_element_type=F32)


def kernel(
    n_src, n_ten, cap,
    tok_hbm, routes_ref, mix_ref, wg_hbm, wu_hbm, wd_hbm, cot_hbm,
    res_ref, gtok_ref, gg_hbm, gu_hbm, gd_hbm,
    tok_ref, cot_ref, wg, wu, wd, pick, x_send, g_send, x_buf, g_buf, hidden, act_a, act_b, dg, du,
    part, part_in, arrived, arrived_in, ret, ret_in, back, back_in, near, near_in, halves, stage,
    w_sem, own_sem, x_ss, x_rs, g_ss, g_rs, xy_ss, xy_rs, gy_ss, gy_rs,
    p_ss, p_rs, q_ss, q_rs, o_ss, o_rs, i_ss, i_rs, f_ss, f_rs, c_ss, c_rs, st_sem,
):
    me = lax.axis_index("expert")
    ten = lax.axis_index("tensor")
    toks, width = tok_ref.shape
    part_w = width // n_ten
    ff = hidden.shape[1]
    tile = 256
    per = n_src // GROUPS
    grp = me // per
    mem = lax.rem(me, per)
    rows_g = per * cap
    partner = [grp, grp + 1 - 2 * lax.rem(grp, 2), lax.rem(grp + 2, 4), 3 - grp]

    def src_rows(s):
        return pl.ds(pl.multiple_of(s * cap, cap), cap)

    def grp_rows(j):
        return pl.ds(pl.multiple_of(partner[j] * rows_g, rows_g), rows_g)

    def members(j, body):
        def step(m, _):
            body(partner[j] * per + lax.rem(mem + m, per))
            return 0

        lax.fori_loop(1 if j == 0 else 0, per, step, 0)

    barrier = pltpu.get_barrier_semaphore()

    def greet(m, _):
        pl.semaphore_signal(
            barrier, inc=1, device_id=(lax.rem(me + m, n_src), ten), device_id_type=MESH
        )
        return 0

    lax.fori_loop(1, n_src, greet, 0)
    for o in range(1, n_ten):
        pl.semaphore_signal(
            barrier, inc=1, device_id=(me, lax.rem(ten + o, n_ten)), device_id_type=MESH
        )

    loads = [
        pltpu.make_async_copy(a, b, w_sem.at[i])
        for i, (a, b) in enumerate((
            (tok_hbm, tok_ref), (cot_hbm, cot_ref), (wg_hbm, wg), (wu_hbm, wu), (wd_hbm, wd)
        ))
    ]
    for load in loads:
        load.start()

    experts = lax.broadcasted_iota(jnp.int32, (128, toks), 0)
    ones = [
        jnp.where(routes_ref[k:k + 1, :] == experts, 1.0, 0.0).astype(F32) for k in range(2)
    ]
    down = lax.broadcasted_iota(jnp.int32, (toks, toks), 0)
    across = lax.broadcasted_iota(jnp.int32, (toks, toks), 1)
    before = jnp.where(down < across, 1.0, 0.0).astype(BF16)
    earlier = dot((ones[0] + ones[1]).astype(BF16), before)
    places = lax.broadcasted_iota(jnp.int32, (n_src * cap, toks), 0)
    place = [
        routes_ref[k:k + 1, :] * cap
        + jnp.sum(ones[k] * earlier, axis=0, keepdims=True).astype(jnp.int32)
        for k in range(2)
    ]
    held = [place[k] == places for k in range(2)]
    spots = (jnp.where(held[0], 1.0, 0.0) + jnp.where(held[1], 1.0, 0.0)).astype(BF16)

    def columns(t):
        return slice(t * part_w, (t + 1) * part_w)

    loads[0].wait()
    for t in range(n_ten):
        x_send[t] = dot(spots, tok_ref[:, columns(t)]).astype(BF16)
    pl.semaphore_wait(barrier, n_src - 1 + n_ten - 1)

    def halves_of(j):
        return slice(None) if j < NEAR else ten

    def to_expert(buf_send, buf, ss, rs, j, e):
        return pltpu.make_async_remote_copy(
            src_ref=buf_send.at[halves_of(j), src_rows(e)],
            dst_ref=buf.at[halves_of(j), src_rows(me)],
            send_sem=ss.at[e], recv_sem=rs.at[me], device_id=(e, ten), device_id_type=MESH,
        )

    def from_source(buf_send, buf, ss, rs, j, s):
        return pltpu.make_async_remote_copy(
            src_ref=buf_send.at[halves_of(j), src_rows(s)],
            dst_ref=buf.at[halves_of(j), src_rows(s)],
            send_sem=ss.at[s], recv_sem=rs.at[s], device_id=(s, ten), device_id_type=MESH,
        )

    def keep_own(buf_send, buf, i):
        own = pltpu.make_async_copy(
            buf_send.at[:, src_rows(me)], buf.at[:, src_rows(me)], own_sem.at[i]
        )
        own.start()
        return own

    def send_to(buf_send, buf, ss, rs, order):
        def to(j, m):
            e = partner[j] * per + lax.rem(mem + m, per)
            to_expert(buf_send, buf, ss, rs, j, e).start()

        def step(m, _):
            for j in order:
                to(j, m)
            return 0

        for j in order:
            if j != 0:
                to(j, 0)
        lax.fori_loop(1, per, step, 0)

    own_x = keep_own(x_send, x_buf, 0)
    send_to(x_send, x_buf, x_ss, x_rs, (2, 0, 3, 1))
    weight = jnp.sum(
        jnp.where(held[0], mix_ref[0:1, :], 0.0) + jnp.where(held[1], mix_ref[1:2, :], 0.0),
        axis=1, keepdims=True,
    )
    loads[1].wait()
    for t in range(n_ten):
        g_send[t] = (weight * dot(spots, cot_ref[:, columns(t)])).astype(BF16)
    own_g = keep_own(g_send, g_buf, 1)

    def upright(row):
        return jnp.sum(jnp.where(down == across, row, 0.0), axis=1, keepdims=True)

    lanes = lax.broadcasted_iota(jnp.int32, (toks, n_src * cap), 1)
    for k in range(2):
        column = upright(place[k].astype(F32)).astype(jnp.int32)
        pick[k] = jnp.where(column == lanes, 1.0, 0.0).astype(BF16)
    mix = [upright(mix_ref[k:k + 1, :]) for k in range(2)]

    def spread(buf, ss, rs, j, o):
        return pltpu.make_async_remote_copy(
            src_ref=buf.at[ten, grp_rows(j)], dst_ref=buf.at[ten, grp_rows(j)],
            send_sem=ss.at[o - 1, j], recv_sem=rs.at[o - 1, j],
            device_id=(me, lax.rem(ten + o, n_ten)), device_id_type=MESH,
        )

    def spread_in(buf, ss, rs, j, o):
        there = lax.rem(ten + n_ten - o, n_ten)
        return pltpu.make_async_remote_copy(
            src_ref=buf.at[ten, grp_rows(j)], dst_ref=buf.at[there, grp_rows(j)],
            send_sem=ss.at[o - 1, j], recv_sem=rs.at[o - 1, j],
            device_id=(me, there), device_id_type=MESH,
        )

    def exchange(buf, land, ss, rs, j, o):
        there = lax.rem(ten + o, n_ten)
        return pltpu.make_async_remote_copy(
            src_ref=buf.at[there, grp_rows(j)], dst_ref=land.at[o - 1, grp_rows(j)],
            send_sem=ss.at[o - 1, j], recv_sem=rs.at[o - 1, j],
            device_id=(me, there), device_id_type=MESH,
        )

    def to_source(buf, out, land, ss, rs, j, s):
        src = buf.at[:, src_rows(s)] if j < NEAR else out.at[src_rows(s)]
        return pltpu.make_async_remote_copy(
            src_ref=src, dst_ref=land.at[halves_of(j), src_rows(me)],
            send_sem=ss.at[s], recv_sem=rs.at[me], device_id=(s, ten), device_id_type=MESH,
        )

    def from_expert(buf, out, land, ss, rs, j, e):
        src = buf.at[:, src_rows(e)] if j < NEAR else out.at[src_rows(e)]
        return pltpu.make_async_remote_copy(
            src_ref=src, dst_ref=land.at[halves_of(j), src_rows(e)],
            send_sem=ss.at[e], recv_sem=rs.at[e], device_id=(e, ten), device_id_type=MESH,
        )

    def take(buf_send, buf, ss, rs, own, ys, yr, j):
        if j == 0:
            own.wait()
        members(j, lambda s: from_source(buf_send, buf, ss, rs, j, s).wait_recv())
        if j >= NEAR:
            for o in range(1, n_ten):
                spread(buf, ys, yr, j, o).start()

    def joined(buf, ys, yr, j):
        if j >= NEAR:
            for o in range(1, n_ten):
                spread_in(buf, ys, yr, j, o).wait_recv()

    own_back = [None, None]

    def give(buf, land, ss, rs, out, final, oss, ors, j, i):
        if j >= NEAR:
            for o in range(1, n_ten):
                exchange(buf, land, ss, rs, j, o).start()
            return
        if j == 0:
            own_back[i] = pltpu.make_async_copy(
                buf.at[:, src_rows(me)], final.at[:, src_rows(me)], own_sem.at[2 + i]
            )
            own_back[i].start()
        members(j, lambda s: to_source(buf, out, final, oss, ors, j, s).start())

    def total_and_return(buf, land, ss, rs, out, final, oss, ors, j):
        for o in range(1, n_ten):
            exchange(buf, land, ss, rs, j, o).wait_recv()
        total = buf[ten, grp_rows(j), :].astype(F32)
        for o in range(1, n_ten):
            total = total + land[o - 1, grp_rows(j), :].astype(F32)
        out[grp_rows(j), :] = total.astype(BF16)
        members(j, lambda s: to_source(buf, out, final, oss, ors, j, s).start())

    def forward(j):
        rows = grp_rows(j)

        def step(n, _):
            cols = pl.ds(pl.multiple_of(n * tile, tile), tile)
            gate = jnp.zeros((rows_g, tile), F32)
            up = jnp.zeros((rows_g, tile), F32)
            for t in range(n_ten):
                deep = slice(t * part_w, (t + 1) * part_w)
                gate = gate + dot(x_buf[t, rows, :], wg[deep, cols])
                up = up + dot(x_buf[t, rows, :], wu[deep, cols])
            sigma = 1.0 / (1.0 + jnp.exp(-gate))
            silu = gate * sigma
            hidden[rows, cols] = (silu * up).astype(BF16)
            act_a[rows, cols] = up * sigma * (1.0 + gate * (1.0 - sigma))
            act_b[rows, cols] = silu
            return 0

        lax.fori_loop(0, ff // tile, step, 0)
        for t in range(n_ten):
            deep = slice(t * part_w, (t + 1) * part_w)
            part[t, rows, :] = dot(hidden[rows, :], wd[:, deep]).astype(BF16)

    def backward(j):
        rows = grp_rows(j)

        def step(n, _):
            cols = pl.ds(pl.multiple_of(n * tile, tile), tile)
            dh = jnp.zeros((rows_g, tile), F32)
            for t in range(n_ten):
                deep = slice(t * part_w, (t + 1) * part_w)
                dh = dh + dot_last(g_buf[t, rows, :], wd[cols, deep])
            dg[rows, cols] = (dh * act_a[rows, cols]).astype(BF16)
            du[rows, cols] = (dh * act_b[rows, cols]).astype(BF16)
            return 0

        lax.fori_loop(0, ff // tile, step, 0)
        for t in range(n_ten):
            deep = slice(t * part_w, (t + 1) * part_w)
            part_in[t, rows, :] = (
                dot_last(dg[rows, :], wg[deep, :]) + dot_last(du[rows, :], wu[deep, :])
            ).astype(BF16)

    out_args = (part, arrived, p_ss, p_rs, ret, back, o_ss, o_rs)
    in_args = (part_in, arrived_in, q_ss, q_rs, ret_in, back_in, i_ss, i_rs)

    for load in loads[2:]:
        load.wait()
    for j in STEPS:
        take(x_send, x_buf, x_ss, x_rs, own_x, xy_ss, xy_rs, j)
        if j == 1:
            send_to(g_send, g_buf, g_ss, g_rs, (2, 3))
        if j == 3:
            send_to(g_send, g_buf, g_ss, g_rs, (0, 1))
        if j >= 1:
            joined(x_buf, xy_ss, xy_rs, j - 1)
            forward(j - 1)
            give(*out_args, j - 1, 0)
    joined(x_buf, xy_ss, xy_rs, 3)
    forward(3)
    give(*out_args, 3, 0)
    total_and_return(*out_args, 2)
    take(g_send, g_buf, g_ss, g_rs, own_g, gy_ss, gy_rs, 0)
    take(g_send, g_buf, g_ss, g_rs, own_g, gy_ss, gy_rs, 1)
    backward(0)
    give(*in_args, 0, 1)
    total_and_return(*out_args, 3)
    take(g_send, g_buf, g_ss, g_rs, own_g, gy_ss, gy_rs, 2)
    backward(1)
    give(*in_args, 1, 1)
    take(g_send, g_buf, g_ss, g_rs, own_g, gy_ss, gy_rs, 3)
    for j in (2, 3):
        joined(g_buf, gy_ss, gy_rs, j)
        backward(j)
        give(*in_args, j, 1)
    total_and_return(*in_args, 2)

    n_stage = ff // tile
    m_stage = width // tile

    def write(slot, dst):
        return pltpu.make_async_copy(stage.at[slot], dst, st_sem.at[slot])

    def grad_x(out_hbm, right, first):
        for m in range(m_stage):
            slot = m % 2
            t, low = (m * tile) // part_w, (m * tile) % part_w
            dst = out_hbm.at[pl.ds(m * tile, tile), :]
            if not (first and m < 2):
                pending[slot].wait()
            stage[slot, :, pl.ds(0, ff)] = dot_first(
                x_buf[t, :, low:low + tile], right[...]
            ).astype(BF16)
            pending[slot] = pltpu.make_async_copy(
                stage.at[slot, :, pl.ds(0, ff)], dst, st_sem.at[slot]
            )
            pending[slot].start()

    pending = [None, None]

    def grad_hidden():
        for m in range(n_stage):
            slot = m % 2
            if pending[slot] is not None:
                pending[slot].wait()
            for t in range(n_ten):
                stage[slot, :, t * part_w:(t + 1) * part_w] = dot_first(
                    hidden[:, m * tile:(m + 1) * tile], g_buf[t]
                ).astype(BF16)
            pending[slot] = write(slot, gd_hbm.at[pl.ds(m * tile, tile), :])
            pending[slot].start()

    def picked(land, weights, j, t):
        rows = grp_rows(j)
        terms = [dot(pick[k, :, rows], land[t, rows, :]) for k in range(2)]
        if weights is not None:
            terms = [weights[k] * terms[k] for k in range(2)]
        return terms[0] + terms[1]

    def swap(i, o):
        there = lax.rem(ten + o, n_ten)
        return pltpu.make_async_remote_copy(
            src_ref=near.at[i, there], dst_ref=near_in.at[i, o - 1],
            send_sem=c_ss.at[i, o - 1], recv_sem=c_rs.at[i, o - 1],
            device_id=(me, there), device_id_type=MESH,
        )

    def gather_near(args, i, weights):
        buf, land, _, _, out, final, oss, ors = args
        own_back[i].wait()
        for j in range(NEAR):
            members(j, lambda e: from_expert(buf, out, final, oss, ors, j, e).wait_recv())
        for t in range(n_ten):
            total = picked(final, weights, 0, t)
            for j in range(1, NEAR):
                total = total + picked(final, weights, j, t)
            near[i, t] = total.astype(BF16)
        for o in range(1, n_ten):
            swap(i, o).start()

    def gather_far(args, i, weights):
        buf, land, _, _, out, final, oss, ors = args
        for o in range(1, n_ten):
            swap(i, o).wait_recv()
        total = near[i, ten].astype(F32)
        for o in range(1, n_ten):
            total = total + near_in[i, o - 1].astype(F32)
        for j in range(NEAR, GROUPS):
            members(j, lambda e: from_expert(buf, out, final, oss, ors, j, e).wait_recv())
            total = total + picked(final, weights, j, ten)
        halves[i, ten] = total.astype(BF16)
        for o in range(1, n_ten):
            share(i, o).start()

    def share(i, o):
        return pltpu.make_async_remote_copy(
            src_ref=halves.at[i, ten], dst_ref=halves.at[i, ten],
            send_sem=f_ss.at[i, o - 1], recv_sem=f_rs.at[i, o - 1],
            device_id=(me, lax.rem(ten + o, n_ten)), device_id_type=MESH,
        )

    def share_in(i, o):
        there = lax.rem(ten + n_ten - o, n_ten)
        return pltpu.make_async_remote_copy(
            src_ref=halves.at[i, ten], dst_ref=halves.at[i, there],
            send_sem=f_ss.at[i, o - 1], recv_sem=f_rs.at[i, o - 1],
            device_id=(me, there), device_id_type=MESH,
        )

    grad_hidden()
    total_and_return(*in_args, 3)
    gather_near(out_args, 0, mix)
    grad_x(gg_hbm, dg, False)
    gather_near(in_args, 1, None)
    gather_far(out_args, 0, mix)
    grad_x(gu_hbm, du, False)
    gather_far(in_args, 1, None)
    for i, out in ((0, res_ref), (1, gtok_ref)):
        for o in range(1, n_ten):
            share_in(i, o).wait_recv()
        for t in range(n_ten):
            out[:, t * part_w:(t + 1) * part_w] = halves[i, t]

    for slot in range(2):
        pending[slot].wait()
    for j in STEPS:
        members(j, lambda e: to_expert(x_send, x_buf, x_ss, x_rs, j, e).wait_send())
        members(j, lambda e: to_expert(g_send, g_buf, g_ss, g_rs, j, e).wait_send())
        for buf, _, _, _, out, final, oss, ors in (out_args, in_args):
            members(j, lambda s: to_source(buf, out, final, oss, ors, j, s).wait_send())
        if j >= NEAR:
            for o in range(1, n_ten):
                spread(x_buf, xy_ss, xy_rs, j, o).wait_send()
                spread(g_buf, gy_ss, gy_rs, j, o).wait_send()
                exchange(part, arrived, p_ss, p_rs, j, o).wait_send()
                exchange(part_in, arrived_in, q_ss, q_rs, j, o).wait_send()
    for i in range(2):
        for o in range(1, n_ten):
            share(i, o).wait_send()
            swap(i, o).wait_send()


def widen_kernel(res_in, gtok_in, gg_in, gu_in, gd_in, res, gtok, gg, gu, gd):
    res[...] = res_in[...]
    gtok[...] = gtok_in[...]
    gg[0] = gg_in[...].astype(F32)
    gu[0] = gu_in[...].astype(F32)
    gd[0] = gd_in[...].astype(F32)


def widened(result, grad_tokens, gg, gu, gd):
    steps = 8
    flat = (result, grad_tokens, gg, gu, gd)

    def block(x):
        return pl.BlockSpec((x.shape[0] // steps, x.shape[1]), lambda i: (i, 0))

    def lifted(x):
        return pl.BlockSpec((1, x.shape[0] // steps, x.shape[1]), lambda i: (0, i, 0))

    return pl.pallas_call(
        widen_kernel,
        grid=(steps,),
        out_shape=tuple(jax.ShapeDtypeStruct(x.shape, BF16) for x in flat[:2])
        + tuple(jax.ShapeDtypeStruct((1,) + x.shape, F32) for x in flat[2:]),
        in_specs=[block(x) for x in flat],
        out_specs=tuple(block(x) for x in flat[:2]) + tuple(lifted(x) for x in flat[2:]),
        compiler_params=pltpu.CompilerParams(vmem_limit_bytes=60 * 2**20),
    )(*flat)


def shards(tokens, routes, mix_weights, w_gate, w_up, w_down, cotangent):
    n_src = lax.axis_size("expert")
    n_ten = lax.axis_size("tensor")
    toks, width = tokens.shape
    ff = w_gate.shape[2]
    cap = 4 * toks // n_src
    rows = n_src * cap
    part_w = width // n_ten
    vmem = pl.BlockSpec(memory_space=pltpu.VMEM)
    hbm = pl.BlockSpec(memory_space=pl.ANY)
    dma = pltpu.SemaphoreType.DMA
    others = n_ten - 1
    scratch = [
        pltpu.VMEM((toks, width), BF16),
        pltpu.VMEM((toks, width), BF16),
        pltpu.VMEM((width, ff), BF16),
        pltpu.VMEM((width, ff), BF16),
        pltpu.VMEM((ff, width), BF16),
        pltpu.VMEM((2, toks, rows), BF16),
        pltpu.VMEM((n_ten, rows, part_w), BF16),
        pltpu.VMEM((n_ten, rows, part_w), BF16),
        pltpu.VMEM((n_ten, rows, part_w), BF16),
        pltpu.VMEM((n_ten, rows, part_w), BF16),
        pltpu.VMEM((rows, ff), BF16),
        pltpu.VMEM((rows, ff), F32),
        pltpu.VMEM((rows, ff), F32),
        pltpu.VMEM((rows, ff), BF16),
        pltpu.VMEM((rows, ff), BF16),
        pltpu.VMEM((n_ten, rows, part_w), BF16),
        pltpu.VMEM((n_ten, rows, part_w), BF16),
        pltpu.VMEM((others, rows, part_w), BF16),
        pltpu.VMEM((others, rows, part_w), BF16),
        pltpu.VMEM((rows, part_w), BF16),
        pltpu.VMEM((rows, part_w), BF16),
        pltpu.VMEM((n_ten, rows, part_w), BF16),
        pltpu.VMEM((n_ten, rows, part_w), BF16),
        pltpu.VMEM((2, n_ten, toks, part_w), BF16),
        pltpu.VMEM((2, others, toks, part_w), BF16),
        pltpu.VMEM((2, n_ten, toks, part_w), BF16),
        pltpu.VMEM((2, 256, width), BF16),
        dma((5,)),
        dma((4,)),
        dma((n_src,)), dma((n_src,)), dma((n_src,)), dma((n_src,)),
        dma((others, GROUPS)), dma((others, GROUPS)), dma((others, GROUPS)), dma((others, GROUPS)),
        dma((others, GROUPS)), dma((others, GROUPS)), dma((others, GROUPS)), dma((others, GROUPS)),
        dma((n_src,)), dma((n_src,)), dma((n_src,)), dma((n_src,)),
        dma((2, others)), dma((2, others)), dma((2, others)), dma((2, others)),
        dma((2,)),
    ]
    result, grad_tokens, gg, gu, gd = pl.pallas_call(
        functools.partial(kernel, n_src, n_ten, cap),
        out_shape=(
            jax.ShapeDtypeStruct((toks, width), BF16),
            jax.ShapeDtypeStruct((toks, width), BF16),
            jax.ShapeDtypeStruct((width, ff), BF16),
            jax.ShapeDtypeStruct((width, ff), BF16),
            jax.ShapeDtypeStruct((ff, width), BF16),
        ),
        in_specs=[hbm, vmem, vmem, hbm, hbm, hbm, hbm],
        out_specs=(vmem, vmem, hbm, hbm, hbm),
        scratch_shapes=scratch,
        compiler_params=pltpu.CompilerParams(
            collective_id=0, has_side_effects=True, vmem_limit_bytes=60 * 2**20
        ),
        cost_estimate=pl.CostEstimate(
            flops=18 * rows * width * ff, bytes_accessed=20 * width * ff,
            transcendentals=rows * ff,
        ),
    )(tokens, routes.T, mix_weights.T, w_gate[0], w_up[0], w_down[0], cotangent)
    return widened(result, grad_tokens, gg, gu, gd)


def solution(mesh):
    in_specs = (
        P("expert", None),
        P("expert", None),
        P("expert", None),
        P("expert", None, "tensor"),
        P("expert", None, "tensor"),
        P("expert", "tensor", None),
        P("expert", None),
    )
    out_specs = (
        P("expert", None),
        P("expert", None),
        P("expert", None, "tensor"),
        P("expert", None, "tensor"),
        P("expert", "tensor", None),
    )
    return jax.shard_map(shards, mesh=mesh, in_specs=in_specs, out_specs=out_specs, check_vma=False)
```

```python
import functools

import jax
import jax.numpy as jnp
from jax import lax
from jax.experimental import pallas as pl
from jax.experimental.pallas import tpu as pltpu
from jax.sharding import PartitionSpec as P

MESH = pl.DeviceIdType.MESH
BF16 = jnp.bfloat16
F32 = jnp.float32
LAST = (((1,), (1,)), ((), ()))
FIRST = (((0,), (0,)), ((), ()))
GROUPS = 4
NEAR_IN = 1
NEAR = 2
STEPS = range(GROUPS)


def dot(a, b):
    return jnp.dot(a, b, preferred_element_type=F32)


def dot_last(a, b):
    return lax.dot_general(a, b, LAST, preferred_element_type=F32)


def dot_first(a, b):
    return lax.dot_general(a, b, FIRST, preferred_element_type=F32)


def kernel(
    n_src, n_ten, cap,
    tok_hbm, routes_ref, mix_ref, wg_hbm, wu_hbm, wd_hbm, cot_hbm,
    res_ref, gtok_ref, gg_hbm, gu_hbm, gd_hbm,
    tok_ref, cot_ref, wg, wu, wd, pick, x_send, g_send, x_buf, g_buf, hidden, act_a, act_b, dg, du,
    part, part_in, arrived, arrived_in, ret, ret_in, back, back_in, near, near_in, halves, stage,
    w_sem, own_sem, x_ss, x_rs, g_ss, g_rs, xy_ss, xy_rs, gy_ss, gy_rs,
    p_ss, p_rs, q_ss, q_rs, o_ss, o_rs, i_ss, i_rs, f_ss, f_rs, c_ss, c_rs, st_sem,
):
    me = lax.axis_index("expert")
    ten = lax.axis_index("tensor")
    toks, width = tok_ref.shape
    part_w = width // n_ten
    ff = hidden.shape[1]
    tile = 256
    per = n_src // GROUPS
    grp = me // per
    mem = lax.rem(me, per)
    rows_g = per * cap
    partner = [grp, grp + 1 - 2 * lax.rem(grp, 2), lax.rem(grp + 2, 4), 3 - grp]

    def src_rows(s):
        return pl.ds(pl.multiple_of(s * cap, cap), cap)

    def grp_rows(j):
        return pl.ds(pl.multiple_of(partner[j] * rows_g, rows_g), rows_g)

    def members(j, body):
        def step(m, _):
            body(partner[j] * per + lax.rem(mem + m, per))
            return 0

        lax.fori_loop(1 if j == 0 else 0, per, step, 0)

    barrier = pltpu.get_barrier_semaphore()

    def greet(m, _):
        pl.semaphore_signal(
            barrier, inc=1, device_id=(lax.rem(me + m, n_src), ten), device_id_type=MESH
        )
        return 0

    lax.fori_loop(1, n_src, greet, 0)
    for o in range(1, n_ten):
        pl.semaphore_signal(
            barrier, inc=1, device_id=(me, lax.rem(ten + o, n_ten)), device_id_type=MESH
        )

    loads = [
        pltpu.make_async_copy(a, b, w_sem.at[i])
        for i, (a, b) in enumerate((
            (tok_hbm, tok_ref), (cot_hbm, cot_ref), (wg_hbm, wg), (wu_hbm, wu), (wd_hbm, wd)
        ))
    ]
    for load in loads:
        load.start()

    experts = lax.broadcasted_iota(jnp.int32, (128, toks), 0)
    ones = [
        jnp.where(routes_ref[k:k + 1, :] == experts, 1.0, 0.0).astype(F32) for k in range(2)
    ]
    down = lax.broadcasted_iota(jnp.int32, (toks, toks), 0)
    across = lax.broadcasted_iota(jnp.int32, (toks, toks), 1)
    before = jnp.where(down < across, 1.0, 0.0).astype(BF16)
    earlier = dot((ones[0] + ones[1]).astype(BF16), before)
    places = lax.broadcasted_iota(jnp.int32, (n_src * cap, toks), 0)
    place = [
        routes_ref[k:k + 1, :] * cap
        + jnp.sum(ones[k] * earlier, axis=0, keepdims=True).astype(jnp.int32)
        for k in range(2)
    ]
    held = [place[k] == places for k in range(2)]
    spots = (jnp.where(held[0], 1.0, 0.0) + jnp.where(held[1], 1.0, 0.0)).astype(BF16)

    def columns(t):
        return slice(t * part_w, (t + 1) * part_w)

    loads[0].wait()
    for t in range(n_ten):
        x_send[t] = dot(spots, tok_ref[:, columns(t)]).astype(BF16)
    pl.semaphore_wait(barrier, n_src - 1 + n_ten - 1)

    def halves_of(j, near=NEAR):
        return slice(None) if j < near else ten

    def to_expert(buf_send, buf, ss, rs, j, e):
        return pltpu.make_async_remote_copy(
            src_ref=buf_send.at[halves_of(j, NEAR_IN), src_rows(e)],
            dst_ref=buf.at[halves_of(j, NEAR_IN), src_rows(me)],
            send_sem=ss.at[e], recv_sem=rs.at[me], device_id=(e, ten), device_id_type=MESH,
        )

    def from_source(buf_send, buf, ss, rs, j, s):
        return pltpu.make_async_remote_copy(
            src_ref=buf_send.at[halves_of(j, NEAR_IN), src_rows(s)],
            dst_ref=buf.at[halves_of(j, NEAR_IN), src_rows(s)],
            send_sem=ss.at[s], recv_sem=rs.at[s], device_id=(s, ten), device_id_type=MESH,
        )

    def keep_own(buf_send, buf, i):
        own = pltpu.make_async_copy(
            buf_send.at[:, src_rows(me)], buf.at[:, src_rows(me)], own_sem.at[i]
        )
        own.start()
        return own

    def send_to(buf_send, buf, ss, rs, order):
        def to(j, m):
            e = partner[j] * per + lax.rem(mem + m, per)
            to_expert(buf_send, buf, ss, rs, j, e).start()

        def step(m, _):
            for j in order:
                to(j, m)
            return 0

        for j in order:
            if j != 0:
                to(j, 0)
        lax.fori_loop(1, per, step, 0)

    own_x = keep_own(x_send, x_buf, 0)
    send_to(x_send, x_buf, x_ss, x_rs, (2, 0, 3, 1))
    weight = jnp.sum(
        jnp.where(held[0], mix_ref[0:1, :], 0.0) + jnp.where(held[1], mix_ref[1:2, :], 0.0),
        axis=1, keepdims=True,
    )
    loads[1].wait()
    for t in range(n_ten):
        g_send[t] = (weight * dot(spots, cot_ref[:, columns(t)])).astype(BF16)
    own_g = keep_own(g_send, g_buf, 1)
    send_to(g_send, g_buf, g_ss, g_rs, (2, 0, 3, 1))

    def upright(row):
        return jnp.sum(jnp.where(down == across, row, 0.0), axis=1, keepdims=True)

    lanes = lax.broadcasted_iota(jnp.int32, (toks, n_src * cap), 1)
    for k in range(2):
        column = upright(place[k].astype(F32)).astype(jnp.int32)
        pick[k] = jnp.where(column == lanes, 1.0, 0.0).astype(BF16)
    mix = [upright(mix_ref[k:k + 1, :]) for k in range(2)]

    def spread(buf, ss, rs, j, o):
        return pltpu.make_async_remote_copy(
            src_ref=buf.at[ten, grp_rows(j)], dst_ref=buf.at[ten, grp_rows(j)],
            send_sem=ss.at[o - 1, j], recv_sem=rs.at[o - 1, j],
            device_id=(me, lax.rem(ten + o, n_ten)), device_id_type=MESH,
        )

    def spread_in(buf, ss, rs, j, o):
        there = lax.rem(ten + n_ten - o, n_ten)
        return pltpu.make_async_remote_copy(
            src_ref=buf.at[ten, grp_rows(j)], dst_ref=buf.at[there, grp_rows(j)],
            send_sem=ss.at[o - 1, j], recv_sem=rs.at[o - 1, j],
            device_id=(me, there), device_id_type=MESH,
        )

    def exchange(buf, land, ss, rs, j, o):
        there = lax.rem(ten + o, n_ten)
        return pltpu.make_async_remote_copy(
            src_ref=buf.at[there, grp_rows(j)], dst_ref=land.at[o - 1, grp_rows(j)],
            send_sem=ss.at[o - 1, j], recv_sem=rs.at[o - 1, j],
            device_id=(me, there), device_id_type=MESH,
        )

    def to_source(buf, out, land, ss, rs, j, s):
        src = buf.at[:, src_rows(s)] if j < NEAR else out.at[src_rows(s)]
        return pltpu.make_async_remote_copy(
            src_ref=src, dst_ref=land.at[halves_of(j), src_rows(me)],
            send_sem=ss.at[s], recv_sem=rs.at[me], device_id=(s, ten), device_id_type=MESH,
        )

    def from_expert(buf, out, land, ss, rs, j, e):
        src = buf.at[:, src_rows(e)] if j < NEAR else out.at[src_rows(e)]
        return pltpu.make_async_remote_copy(
            src_ref=src, dst_ref=land.at[halves_of(j), src_rows(e)],
            send_sem=ss.at[e], recv_sem=rs.at[e], device_id=(e, ten), device_id_type=MESH,
        )

    def take(buf_send, buf, ss, rs, own, ys, yr, j):
        if j == 0:
            own.wait()
        members(j, lambda s: from_source(buf_send, buf, ss, rs, j, s).wait_recv())
        if j >= NEAR_IN:
            for o in range(1, n_ten):
                spread(buf, ys, yr, j, o).start()

    def joined(buf, ys, yr, j):
        if j >= NEAR_IN:
            for o in range(1, n_ten):
                spread_in(buf, ys, yr, j, o).wait_recv()

    own_back = [None, None]

    def give(buf, land, ss, rs, out, final, oss, ors, j, i):
        if j >= NEAR:
            for o in range(1, n_ten):
                exchange(buf, land, ss, rs, j, o).start()
            return
        if j == 0:
            own_back[i] = pltpu.make_async_copy(
                buf.at[:, src_rows(me)], final.at[:, src_rows(me)], own_sem.at[2 + i]
            )
            own_back[i].start()
        members(j, lambda s: to_source(buf, out, final, oss, ors, j, s).start())

    def total_and_return(buf, land, ss, rs, out, final, oss, ors, j):
        for o in range(1, n_ten):
            exchange(buf, land, ss, rs, j, o).wait_recv()
        total = buf[ten, grp_rows(j), :].astype(F32)
        for o in range(1, n_ten):
            total = total + land[o - 1, grp_rows(j), :].astype(F32)
        out[grp_rows(j), :] = total.astype(BF16)
        members(j, lambda s: to_source(buf, out, final, oss, ors, j, s).start())

    def forward(j):
        rows = grp_rows(j)

        def step(n, _):
            cols = pl.ds(pl.multiple_of(n * tile, tile), tile)
            gate = jnp.zeros((rows_g, tile), F32)
            up = jnp.zeros((rows_g, tile), F32)
            for t in range(n_ten):
                deep = slice(t * part_w, (t + 1) * part_w)
                gate = gate + dot(x_buf[t, rows, :], wg[deep, cols])
                up = up + dot(x_buf[t, rows, :], wu[deep, cols])
            sigma = 1.0 / (1.0 + jnp.exp(-gate))
            silu = gate * sigma
            hidden[rows, cols] = (silu * up).astype(BF16)
            act_a[rows, cols] = up * sigma * (1.0 + gate * (1.0 - sigma))
            act_b[rows, cols] = silu
            return 0

        lax.fori_loop(0, ff // tile, step, 0)
        for t in range(n_ten):
            deep = slice(t * part_w, (t + 1) * part_w)
            part[t, rows, :] = dot(hidden[rows, :], wd[:, deep]).astype(BF16)

    def backward(j):
        rows = grp_rows(j)

        def step(n, _):
            cols = pl.ds(pl.multiple_of(n * tile, tile), tile)
            dh = jnp.zeros((rows_g, tile), F32)
            for t in range(n_ten):
                deep = slice(t * part_w, (t + 1) * part_w)
                dh = dh + dot_last(g_buf[t, rows, :], wd[cols, deep])
            dg[rows, cols] = (dh * act_a[rows, cols]).astype(BF16)
            du[rows, cols] = (dh * act_b[rows, cols]).astype(BF16)
            return 0

        lax.fori_loop(0, ff // tile, step, 0)
        for t in range(n_ten):
            deep = slice(t * part_w, (t + 1) * part_w)
            part_in[t, rows, :] = (
                dot_last(dg[rows, :], wg[deep, :]) + dot_last(du[rows, :], wu[deep, :])
            ).astype(BF16)

    out_args = (part, arrived, p_ss, p_rs, ret, back, o_ss, o_rs)
    in_args = (part_in, arrived_in, q_ss, q_rs, ret_in, back_in, i_ss, i_rs)

    for load in loads[2:]:
        load.wait()
    for j in STEPS:
        take(x_send, x_buf, x_ss, x_rs, own_x, xy_ss, xy_rs, j)
        if j >= 1:
            joined(x_buf, xy_ss, xy_rs, j - 1)
            forward(j - 1)
            give(*out_args, j - 1, 0)
    joined(x_buf, xy_ss, xy_rs, 3)
    forward(3)
    give(*out_args, 3, 0)
    total_and_return(*out_args, 2)
    take(g_send, g_buf, g_ss, g_rs, own_g, gy_ss, gy_rs, 0)
    take(g_send, g_buf, g_ss, g_rs, own_g, gy_ss, gy_rs, 1)
    backward(0)
    give(*in_args, 0, 1)
    total_and_return(*out_args, 3)
    take(g_send, g_buf, g_ss, g_rs, own_g, gy_ss, gy_rs, 2)
    joined(g_buf, gy_ss, gy_rs, 1)
    backward(1)
    give(*in_args, 1, 1)
    take(g_send, g_buf, g_ss, g_rs, own_g, gy_ss, gy_rs, 3)
    for j in (2, 3):
        joined(g_buf, gy_ss, gy_rs, j)
        backward(j)
        give(*in_args, j, 1)
    total_and_return(*in_args, 2)

    n_stage = ff // tile
    m_stage = width // tile

    def write(slot, dst):
        return pltpu.make_async_copy(stage.at[slot], dst, st_sem.at[slot])

    def grad_x(out_hbm, right, first):
        for m in range(m_stage):
            slot = m % 2
            t, low = (m * tile) // part_w, (m * tile) % part_w
            dst = out_hbm.at[pl.ds(m * tile, tile), :]
            if not (first and m < 2):
                pending[slot].wait()
            stage[slot, :, pl.ds(0, ff)] = dot_first(
                x_buf[t, :, low:low + tile], right[...]
            ).astype(BF16)
            pending[slot] = pltpu.make_async_copy(
                stage.at[slot, :, pl.ds(0, ff)], dst, st_sem.at[slot]
            )
            pending[slot].start()

    pending = [None, None]

    def grad_hidden():
        for m in range(n_stage):
            slot = m % 2
            if pending[slot] is not None:
                pending[slot].wait()
            for t in range(n_ten):
                stage[slot, :, t * part_w:(t + 1) * part_w] = dot_first(
                    hidden[:, m * tile:(m + 1) * tile], g_buf[t]
                ).astype(BF16)
            pending[slot] = write(slot, gd_hbm.at[pl.ds(m * tile, tile), :])
            pending[slot].start()

    def picked(land, weights, j, t):
        rows = grp_rows(j)
        terms = [dot(pick[k, :, rows], land[t, rows, :]) for k in range(2)]
        if weights is not None:
            terms = [weights[k] * terms[k] for k in range(2)]
        return terms[0] + terms[1]

    def swap(i, o):
        there = lax.rem(ten + o, n_ten)
        return pltpu.make_async_remote_copy(
            src_ref=near.at[i, there], dst_ref=near_in.at[i, o - 1],
            send_sem=c_ss.at[i, o - 1], recv_sem=c_rs.at[i, o - 1],
            device_id=(me, there), device_id_type=MESH,
        )

    def gather_near(args, i, weights):
        buf, land, _, _, out, final, oss, ors = args
        own_back[i].wait()
        for j in range(NEAR):
            members(j, lambda e: from_expert(buf, out, final, oss, ors, j, e).wait_recv())
        for t in range(n_ten):
            total = picked(final, weights, 0, t)
            for j in range(1, NEAR):
                total = total + picked(final, weights, j, t)
            near[i, t] = total.astype(BF16)
        for o in range(1, n_ten):
            swap(i, o).start()

    def gather_far(args, i, weights):
        buf, land, _, _, out, final, oss, ors = args
        for o in range(1, n_ten):
            swap(i, o).wait_recv()
        total = near[i, ten].astype(F32)
        for o in range(1, n_ten):
            total = total + near_in[i, o - 1].astype(F32)
        for j in range(NEAR, GROUPS):
            members(j, lambda e: from_expert(buf, out, final, oss, ors, j, e).wait_recv())
            total = total + picked(final, weights, j, ten)
        return total.astype(BF16)

    def share(o):
        return pltpu.make_async_remote_copy(
            src_ref=halves.at[ten], dst_ref=halves.at[ten],
            send_sem=f_ss.at[o - 1], recv_sem=f_rs.at[o - 1],
            device_id=(me, lax.rem(ten + o, n_ten)), device_id_type=MESH,
        )

    def share_in(o):
        there = lax.rem(ten + n_ten - o, n_ten)
        return pltpu.make_async_remote_copy(
            src_ref=halves.at[ten], dst_ref=halves.at[there],
            send_sem=f_ss.at[o - 1], recv_sem=f_rs.at[o - 1],
            device_id=(me, there), device_id_type=MESH,
        )

    grad_hidden()
    total_and_return(*in_args, 3)
    gather_near(out_args, 0, mix)
    grad_x(gg_hbm, dg, False)
    gather_near(in_args, 1, None)
    halves[ten] = gather_far(out_args, 0, mix)
    for o in range(1, n_ten):
        share(o).start()
    grad_x(gu_hbm, du, False)
    gtok_ref[...] = gather_far(in_args, 1, None)
    for o in range(1, n_ten):
        share_in(o).wait_recv()
    for t in range(n_ten):
        res_ref[:, columns(t)] = halves[t]

    for slot in range(2):
        pending[slot].wait()
    for j in STEPS:
        members(j, lambda e: to_expert(x_send, x_buf, x_ss, x_rs, j, e).wait_send())
        members(j, lambda e: to_expert(g_send, g_buf, g_ss, g_rs, j, e).wait_send())
        for buf, _, _, _, out, final, oss, ors in (out_args, in_args):
            members(j, lambda s: to_source(buf, out, final, oss, ors, j, s).wait_send())
        if j >= NEAR_IN:
            for o in range(1, n_ten):
                spread(x_buf, xy_ss, xy_rs, j, o).wait_send()
                spread(g_buf, gy_ss, gy_rs, j, o).wait_send()
        if j >= NEAR:
            for o in range(1, n_ten):
                exchange(part, arrived, p_ss, p_rs, j, o).wait_send()
                exchange(part_in, arrived_in, q_ss, q_rs, j, o).wait_send()
    for i in range(2):
        for o in range(1, n_ten):
            swap(i, o).wait_send()
    for o in range(1, n_ten):
        share(o).wait_send()


def widen_kernel(res_in, gg_in, gu_in, gd_in, res, gg, gu, gd):
    res[...] = res_in[...]
    gg[0] = gg_in[...].astype(F32)
    gu[0] = gu_in[...].astype(F32)
    gd[0] = gd_in[...].astype(F32)


def widened(result, gg, gu, gd):
    steps = 8
    flat = (result, gg, gu, gd)

    def block(x):
        return pl.BlockSpec((x.shape[0] // steps, x.shape[1]), lambda i: (i, 0))

    def lifted(x):
        return pl.BlockSpec((1, x.shape[0] // steps, x.shape[1]), lambda i: (0, i, 0))

    return pl.pallas_call(
        widen_kernel,
        grid=(steps,),
        out_shape=(jax.ShapeDtypeStruct(result.shape, BF16),)
        + tuple(jax.ShapeDtypeStruct((1,) + x.shape, F32) for x in flat[1:]),
        in_specs=[block(x) for x in flat],
        out_specs=(block(result),) + tuple(lifted(x) for x in flat[1:]),
        compiler_params=pltpu.CompilerParams(vmem_limit_bytes=60 * 2**20),
        cost_estimate=pl.CostEstimate(
            flops=3 * gg.size, bytes_accessed=18 * gg.size, transcendentals=0
        ),
    )(*flat)


def shards(tokens, routes, mix_weights, w_gate, w_up, w_down, cotangent):
    n_src = lax.axis_size("expert")
    n_ten = lax.axis_size("tensor")
    toks, width = tokens.shape
    ff = w_gate.shape[2]
    cap = 4 * toks // n_src
    rows = n_src * cap
    part_w = width // n_ten
    vmem = pl.BlockSpec(memory_space=pltpu.VMEM)
    hbm = pl.BlockSpec(memory_space=pl.ANY)
    dma = pltpu.SemaphoreType.DMA
    others = n_ten - 1
    scratch = [
        pltpu.VMEM((toks, width), BF16),
        pltpu.VMEM((toks, width), BF16),
        pltpu.VMEM((width, ff), BF16),
        pltpu.VMEM((width, ff), BF16),
        pltpu.VMEM((ff, width), BF16),
        pltpu.VMEM((2, toks, rows), BF16),
        pltpu.VMEM((n_ten, rows, part_w), BF16),
        pltpu.VMEM((n_ten, rows, part_w), BF16),
        pltpu.VMEM((n_ten, rows, part_w), BF16),
        pltpu.VMEM((n_ten, rows, part_w), BF16),
        pltpu.VMEM((rows, ff), BF16),
        pltpu.VMEM((rows, ff), F32),
        pltpu.VMEM((rows, ff), F32),
        pltpu.VMEM((rows, ff), BF16),
        pltpu.VMEM((rows, ff), BF16),
        pltpu.VMEM((n_ten, rows, part_w), BF16),
        pltpu.VMEM((n_ten, rows, part_w), BF16),
        pltpu.VMEM((others, rows, part_w), BF16),
        pltpu.VMEM((others, rows, part_w), BF16),
        pltpu.VMEM((rows, part_w), BF16),
        pltpu.VMEM((rows, part_w), BF16),
        pltpu.VMEM((n_ten, rows, part_w), BF16),
        pltpu.VMEM((n_ten, rows, part_w), BF16),
        pltpu.VMEM((2, n_ten, toks, part_w), BF16),
        pltpu.VMEM((2, others, toks, part_w), BF16),
        pltpu.VMEM((n_ten, toks, part_w), BF16),
        pltpu.VMEM((2, 256, width), BF16),
        dma((5,)),
        dma((4,)),
        dma((n_src,)), dma((n_src,)), dma((n_src,)), dma((n_src,)),
        dma((others, GROUPS)), dma((others, GROUPS)), dma((others, GROUPS)), dma((others, GROUPS)),
        dma((others, GROUPS)), dma((others, GROUPS)), dma((others, GROUPS)), dma((others, GROUPS)),
        dma((n_src,)), dma((n_src,)), dma((n_src,)), dma((n_src,)),
        dma((others,)), dma((others,)), dma((2, others)), dma((2, others)),
        dma((2,)),
    ]
    result, mine, gg, gu, gd = pl.pallas_call(
        functools.partial(kernel, n_src, n_ten, cap),
        out_shape=(
            jax.ShapeDtypeStruct((toks, width), BF16),
            jax.ShapeDtypeStruct((toks, part_w), BF16),
            jax.ShapeDtypeStruct((width, ff), BF16),
            jax.ShapeDtypeStruct((width, ff), BF16),
            jax.ShapeDtypeStruct((ff, width), BF16),
        ),
        in_specs=[hbm, vmem, vmem, hbm, hbm, hbm, hbm],
        out_specs=(vmem, vmem, hbm, hbm, hbm),
        scratch_shapes=scratch,
        compiler_params=pltpu.CompilerParams(
            collective_id=0, has_side_effects=True, vmem_limit_bytes=60 * 2**20
        ),
        cost_estimate=pl.CostEstimate(
            flops=18 * rows * width * ff, bytes_accessed=20 * width * ff,
            transcendentals=rows * ff,
        ),
    )(tokens, routes.T, mix_weights.T, w_gate[0], w_up[0], w_down[0], cotangent)
    ten = lax.axis_index("tensor")
    held = [mine] + [
        lax.ppermute(mine, "tensor", [(t, (t + o) % n_ten) for t in range(n_ten)])
        for o in range(1, n_ten)
    ]
    result, gg, gu, gd = widened(result, gg, gu, gd)
    parts = []
    for t in range(n_ten):
        part = held[0]
        for o in range(1, n_ten):
            part = jnp.where(lax.rem(ten + n_ten - o, n_ten) == t, held[o], part)
        parts.append(part)
    return result, jnp.concatenate(parts, axis=1), gg, gu, gd


def solution(mesh):
    in_specs = (
        P("expert", None),
        P("expert", None),
        P("expert", None),
        P("expert", None, "tensor"),
        P("expert", None, "tensor"),
        P("expert", "tensor", None),
        P("expert", None),
    )
    out_specs = (
        P("expert", None),
        P("expert", None),
        P("expert", None, "tensor"),
        P("expert", None, "tensor"),
        P("expert", "tensor", None),
    )
    return jax.shard_map(shards, mesh=mesh, in_specs=in_specs, out_specs=out_specs, check_vma=False)
```
